32 devices in a mesh: row: 4 (over x, core), col: 8 (over z, y).
Axes of the slice: x: 2, y: 2, z: 4, core: 2. Of those that a mesh axis runs over, the one named last changes fastest.
Arguments:
- specimen: float32 [2, 512, 2048], P(None, 'row', 'col'), may hold values from -6 to 6
- probe_field: float32 [2, 256, 256], replicated, may hold values from -6 to 6
- scan_offsets: int32 [4, 8, 2, 2], replicated, may hold values from -128 to 128, as said below
- live_counts: int32 [4, 8], replicated, may hold values from 1 to 2, as said below
- magnitudes: float32 [4, 8, 2, 256, 256], P('row', 'col'), may hold values from 0 to 2
Outputs:
- specimen_next: float32 [2, 512, 2048], P(None, 'row', 'col')
- probe_next: float32 [2, 256, 256], replicated
The draws below stay inside these ranges and needn't reach their ends.
Inputs may be any that keep to these rules, and one draw needn't show every extreme that they name: `scan_offsets`: rows of a patch start within -128 to 0 of the tile's first row, columns within -128 to 128 of its first column. Tile (a, b) owns the positions in its first live_counts[a, b] slots.
All inputs are finite; a program needn't handle non-finite values.
Results may differ from the reference program's by a relative error of at most 0.0003.
Values sent between devices are 32-bit elements; how exact they have to be, the bound alone decides.
No kernel may reach another device: no remote copies, remote signals or barrier semaphores. Data moves between devices by JAX's collectives and lax.ppermute only.
A program may use at most 64 MiB of HBM per device.

```python
import jax
import jax.numpy as jnp
from jax import lax

PROBE = 256
TILE_R = 128
TILE_C = 256
POS_DEV = 2
NY = 512
NX = 2048


def draw_scan_offsets(key, part):
    grid_rows = NY // TILE_R
    grid_cols = NX // TILE_C
    half = PROBE // 2
    key_rows, key_cols, key_pick = jax.random.split(jax.random.fold_in(key, 11), 3)
    shape_here = (grid_rows, grid_cols, POS_DEV)
    row_offsets = jax.random.randint(key_rows, shape_here, -half, TILE_R - half + 1)
    col_offsets = jax.random.randint(key_cols, shape_here, -half, TILE_C - half + 1)
    entries = grid_rows * grid_cols * POS_DEV
    lowest = jax.random.randint(key_pick, (), 0, entries)
    highest = (lowest + 1) % entries
    flat_index = jnp.arange(entries, dtype=jnp.int32).reshape(shape_here)
    row_offsets = jnp.where(flat_index == lowest, -half, jnp.where(flat_index == highest, TILE_R - half, row_offsets))
    col_offsets = jnp.where(flat_index == lowest, -half, jnp.where(flat_index == highest, TILE_C - half, col_offsets))
    return jnp.stack([row_offsets, col_offsets], -1).astype(jnp.int32)


def draw_live_counts(key, part):
    grid_rows = NY // TILE_R
    grid_cols = NX // TILE_C
    key_counts, key_pick = jax.random.split(jax.random.fold_in(key, 23), 2)
    counts = jax.random.randint(key_counts, (grid_rows, grid_cols), 1, POS_DEV + 1)
    entries = grid_rows * grid_cols
    fullest = jax.random.randint(key_pick, (), 0, entries)
    emptiest = (fullest + 1) % entries
    flat_index = jnp.arange(entries, dtype=jnp.int32).reshape((grid_rows, grid_cols))
    counts = jnp.where(flat_index == fullest, POS_DEV, jnp.where(flat_index == emptiest, 1, counts))
    return counts.astype(jnp.int32)


def block_levels(stream_key, dims, cuts, smallest, largest):
    def one(axis_at, shards_of):
        steps = jax.random.uniform(jax.random.fold_in(jax.random.fold_in(stream_key, 6), axis_at), (shards_of,), jnp.float32, smallest / len(cuts), largest / len(cuts))
        return jnp.repeat(jnp.exp(steps), dims[axis_at] // shards_of).reshape((-1,) + (1,) * (len(dims) - axis_at - 1))

    factor_of = one(*cuts[0])
    for cut in cuts[1:]:
        factor_of = factor_of * one(*cut)
    return factor_of


def gaussian(own_key, dims, deviation, bound, cuts=(), kind=jnp.bfloat16):
    factor_of = block_levels(own_key, dims, cuts, -0.22, 0.18) if cuts else 1.0
    values = jax.random.normal(own_key, dims, jnp.float32) * deviation * factor_of
    return jnp.minimum(jnp.maximum(values, -bound), bound).astype(kind)


def setup_inputs(seed: int = 0) -> dict:
    key_list = jax.random.split(jax.random.key(seed), 6)
    specimen = gaussian(key_list[0], (2, NY, NX), 1.0, 6.0, ((1, 4), (2, 8)), jnp.float32)
    probe_field = gaussian(key_list[1], (2, PROBE, PROBE), 1.0, 6.0, (), jnp.float32)
    scan_offsets = draw_scan_offsets(jax.random.fold_in(key_list[5], 71), 0)
    live_counts = draw_live_counts(jax.random.fold_in(key_list[5], 71), 0)
    magnitudes = jnp.clip(2.0 * jax.random.uniform(key_list[4], (NY // TILE_R, NX // TILE_C, POS_DEV, PROBE, PROBE), jnp.float32) ** block_levels(key_list[4], (NY // TILE_R, NX // TILE_C, POS_DEV, PROBE, PROBE), ((0, 4), (1, 8)), -0.2, 0.2), 0.0, 2.0)
    return {"specimen": specimen, "probe_field": probe_field, "scan_offsets": scan_offsets, "live_counts": live_counts, "magnitudes": magnitudes}


modulus_floor = 0.25
object_damping = 0.1
probe_damping = 0.1

def transform(wave_real, wave_imag, inverse):
    field = lax.complex(wave_real, wave_imag)
    if inverse:
        result = jnp.fft.ifft2(field, norm='ortho')
    else:
        result = jnp.fft.fft2(field, norm='ortho')
    return (jnp.real(result), jnp.imag(result))

def reference(specimen, probe_field, scan_offsets, live_counts, magnitudes):
    half = PROBE // 2
    grid_rows = specimen.shape[1] // TILE_R
    grid_cols = specimen.shape[2] // TILE_C
    padded = jnp.pad(specimen, ((0, 0), (half, half), (half, half)))
    probe_real = probe_field[0]
    probe_imag = probe_field[1]
    power = probe_real * probe_real + probe_imag * probe_imag
    slot_ids = jnp.arange(POS_DEV, dtype=jnp.int32)
    zero_index = jnp.zeros((), jnp.int32)

    def tile_step(carry, tile):
        buffer, probe_sums = carry
        tile_row = tile // grid_cols
        tile_col = tile % grid_cols
        offsets_here = scan_offsets[tile_row, tile_col]
        live = (slot_ids < live_counts[tile_row, tile_col]).astype(jnp.float32)[:, None, None]
        row_starts = (tile_row * TILE_R + offsets_here[:, 0] + half).astype(jnp.int32)
        col_starts = (tile_col * TILE_C + offsets_here[:, 1] + half).astype(jnp.int32)

        def extract(row_start, col_start):
            return lax.dynamic_slice(padded, (zero_index, row_start, col_start), (2, PROBE, PROBE))
        patches = jax.vmap(extract)(row_starts, col_starts)
        patch_real = patches[:, 0]
        patch_imag = patches[:, 1]
        measured = magnitudes[tile_row, tile_col]
        wave_real = probe_real * patch_real - probe_imag * patch_imag
        wave_imag = probe_real * patch_imag + probe_imag * patch_real
        far_real, far_imag = transform(wave_real, wave_imag, False)
        modulus = jnp.sqrt(far_real * far_real + far_imag * far_imag)
        factor = measured / jnp.maximum(modulus, modulus_floor) - 1.0
        diff_real, diff_imag = transform(far_real * factor, far_imag * factor, True)
        diff_real = diff_real * live
        diff_imag = diff_imag * live
        grad_real = probe_real * diff_real + probe_imag * diff_imag
        grad_imag = probe_real * diff_imag - probe_imag * diff_real
        pieces = jnp.stack([grad_real, grad_imag, live * power], axis=1)

        def place(slot, total):
            start = (zero_index, row_starts[slot], col_starts[slot])
            current = lax.dynamic_slice(total, start, (3, PROBE, PROBE))
            return lax.dynamic_update_slice(total, current + pieces[slot], start)
        buffer = lax.fori_loop(0, POS_DEV, place, buffer)
        probe_terms = jnp.stack([lax.optimization_barrier(jnp.sum(patch_real * diff_real + patch_imag * diff_imag, 0)), lax.optimization_barrier(jnp.sum(patch_real * diff_imag - patch_imag * diff_real, 0)), lax.optimization_barrier(jnp.sum(live * (patch_real * patch_real + patch_imag * patch_imag), 0))])
        return ((buffer, probe_sums + probe_terms), None)
    start_buffer = jnp.zeros((3, padded.shape[1], padded.shape[2]), jnp.float32)
    start_probe = jnp.zeros((3, PROBE, PROBE), jnp.float32)
    tiles = jnp.arange(grid_rows * grid_cols, dtype=jnp.int32)
    (buffer, probe_sums), unused = lax.scan(tile_step, (start_buffer, start_probe), tiles)
    inner = buffer[:, half:half + specimen.shape[1], half:half + specimen.shape[2]]
    damping = object_damping * jnp.max(power)
    specimen_next = specimen + inner[:2] / (inner[2] + damping)
    weight = probe_sums[2]
    probe_next = probe_field + probe_sums[:2] / (weight + probe_damping * jnp.mean(weight))
    return (specimen_next, probe_next)
```

```python
import functools
import math

import jax
import jax.numpy as jnp
import ml_dtypes
import numpy as np
from jax import lax
from jax.experimental import pallas as pl
from jax.experimental.pallas import tpu as pltpu
from jax.sharding import PartitionSpec as P

modulus_floor = 0.25
object_damping = 0.1
probe_damping = 0.1
LANES = 128
SUBLANES = 8
VMEM_LIMIT = 48 * 1024 * 1024


def split_table(table):
    high = table.astype(ml_dtypes.bfloat16)
    low = (table - high.astype(np.float64)).astype(ml_dtypes.bfloat16)
    return np.stack([high, low])


def dft_tables(width):
    counter = np.arange(width)
    angle = (counter[:, None] * counter[None, :] % width) * (2.0 * math.pi / width)
    cosine = np.cos(angle) / math.sqrt(width)
    sine = np.sin(angle) / math.sqrt(width)
    turn = np.block([[cosine, -sine], [sine, cosine]])
    return split_table(turn), split_table(turn.T)


def halves(value):
    high = value.astype(jnp.bfloat16)
    return high, (value - high.astype(jnp.float32)).astype(jnp.bfloat16)


def product(left, right):
    dot = functools.partial(jnp.dot, preferred_element_type=jnp.float32)
    return dot(left[0], right[0]) + (dot(left[1], right[0]) + dot(left[0], right[1]))


def split_start(start, step, last):
    aligned = jnp.minimum(start // step, last // step) * step
    return pl.multiple_of(aligned, step), start - aligned


def lane_groups(value):
    return [value[..., at : at + LANES] for at in range(0, value.shape[-1], LANES)]


def cut(value, row_shift, lane_shift):
    rows, lanes = value.shape
    value = value.reshape(rows // SUBLANES, SUBLANES, lanes)
    lane_turn = lax.rem(LANES - lane_shift, LANES)
    row_turn = lax.rem(SUBLANES - row_shift, SUBLANES)
    shape = (rows // SUBLANES, SUBLANES, LANES)
    keep_lane = lax.broadcasted_iota(jnp.int32, shape, 2) < LANES - lane_shift
    keep_row = lax.broadcasted_iota(jnp.int32, shape, 1)[1:] < SUBLANES - row_shift
    turned = [pltpu.roll(group, lane_turn, 2) for group in lane_groups(value)]
    parts = []
    for first, second in zip(turned[:-1], turned[1:]):
        part = pltpu.roll(jnp.where(keep_lane, first, second), row_turn, 1)
        part = jnp.where(keep_row, part[:-1], part[1:])
        parts.append(part.reshape(rows - SUBLANES, LANES))
    return jnp.concatenate(parts, 1)


def spread(value, row_shift, lane_shift):
    rows, lanes = value.shape
    value = value.reshape(rows // SUBLANES, SUBLANES, lanes)
    shape = (rows // SUBLANES + 1, SUBLANES, LANES)
    lane_turn = lax.rem(lane_shift, LANES)
    take_lane = lax.broadcasted_iota(jnp.int32, shape, 2) < lane_shift
    take_row = lax.broadcasted_iota(jnp.int32, shape, 1) < row_shift
    blank_row = jnp.zeros((1, SUBLANES, LANES), value.dtype)
    turned = []
    for group in lane_groups(value):
        group = pltpu.roll(group, row_shift, 1)
        group = jnp.where(
            take_row,
            jnp.concatenate([blank_row, group], 0),
            jnp.concatenate([group, blank_row], 0),
        )
        turned.append(pltpu.roll(group, lane_turn, 2))
    blank = jnp.zeros(shape, value.dtype)
    parts = [
        jnp.where(take_lane, first, second).reshape(rows + SUBLANES, LANES)
        for first, second in zip([blank] + turned, turned + [blank])
    ]
    return jnp.concatenate(parts, 1)


def lighting_kernel(offsets, counts, probe, out, pad):
    rows, cols, slots = offsets.shape[:3]
    tile_r, tile_c = out.shape
    width = probe.shape[1]
    half = width // 2
    row_place = lax.axis_index("row")
    col_place = lax.axis_index("col")
    power = probe[0] * probe[0] + probe[1] * probe[1]
    pad[...] = jnp.zeros_like(pad)
    pad[tile_r : tile_r + width, tile_c : tile_c + width] = power
    out[...] = jnp.full(out.shape, object_damping * jnp.max(power))
    wide = tile_c + LANES
    for row_step in (-1, 0, 1):
        for col_step in (-1, 0, 1):
            row, col = row_place + row_step, col_place + col_step
            inside = (row >= 0) & (row < rows) & (col >= 0) & (col < cols)
            row_at = jnp.clip(row, 0, rows - 1)
            col_at = jnp.clip(col, 0, cols - 1)
            for slot in range(slots):
                top = offsets[row_at, col_at, slot, 0] + row_step * tile_r
                left = offsets[row_at, col_at, slot, 1] + col_step * tile_c

                @pl.when(
                    inside
                    & (slot < counts[row_at, col_at])
                    & (left > -width)
                    & (left < tile_c)
                )
                def _():
                    row, row_shift = split_start(tile_r - top, SUBLANES, tile_r + width)
                    lane, lane_shift = split_start(tile_c - left, LANES, pad.shape[1] - wide)
                    part = pad[pl.ds(row, tile_r + SUBLANES), pl.ds(lane, wide)]
                    out[...] += cut(part, row_shift, lane_shift)


def lighting(offsets, counts, probe, tile_r, tile_c):
    width = probe.shape[1]
    smem = pl.BlockSpec(memory_space=pltpu.SMEM)
    vmem = pl.BlockSpec(memory_space=pltpu.VMEM)
    return pl.pallas_call(
        lighting_kernel,
        out_shape=jax.ShapeDtypeStruct((tile_r, tile_c), jnp.float32),
        in_specs=[smem, smem, vmem],
        out_specs=vmem,
        scratch_shapes=[
            pltpu.VMEM((2 * tile_r + width + SUBLANES, 2 * tile_c + width), jnp.float32)
        ],
        compiler_params=pltpu.CompilerParams(vmem_limit_bytes=VMEM_LIMIT),
        cost_estimate=pl.CostEstimate(flops=4000000, bytes_accessed=800000, transcendentals=0),
    )(offsets, counts, probe)


def update_kernel(
    offsets, counts, probe, magnitudes, table, table_t, own, rim, near, near_rim, far, far_rim,
    terms, total, above, center, below, ext, patches, left, right,
):
    slots, width = magnitudes.shape[0], magnitudes.shape[1]
    half = width // 2
    tile_r, tile_c = own.shape[1:]
    row_place = lax.axis_index("row")
    col_place = lax.axis_index("col")
    row_odd = lax.rem(row_place, 2)
    col_odd = lax.rem(col_place, 2)
    near_row = pl.multiple_of((1 - row_odd) * (tile_r + half), half)
    far_row = pl.multiple_of(row_odd * (tile_r + half), half)
    pair_col = pl.multiple_of((1 - col_odd) * (tile_c + half), half)
    other_col = pl.multiple_of(col_odd * (tile_c + half), half)
    for part in range(2):
        for rows, mid, edge in ((half, own, rim), (near_row, near, near_rim), (far_row, far, far_rim)):
            at = pl.ds(rows, tile_r)
            ext[part, at, half : half + tile_c] = mid[part]
            ext[part, at, pl.ds(pair_col, half)] = edge[0, part]
            ext[part, at, pl.ds(other_col, half)] = edge[1, part]
    wide = width + LANES
    live_count = counts[row_place, col_place]
    places = []
    for slot in range(slots):
        row, row_shift = split_start(
            offsets[row_place, col_place, slot, 0] + half, SUBLANES, tile_r
        )
        lane, lane_shift = split_start(
            offsets[row_place, col_place, slot, 1] + half, LANES, 2 * half - LANES
        )
        block = (pl.ds(row, width + SUBLANES), pl.ds(lane, wide))
        places.append((block, row_shift, lane_shift))
        for part in range(2):
            patches[slot, part] = cut(ext[part, *block], row_shift, lane_shift)
    probe_real, probe_imag = probe[0], probe[1]
    for slot in range(slots):
        patch_real, patch_imag = patches[slot, 0], patches[slot, 1]
        at = slice(slot * width, (slot + 1) * width)
        for part, wave in enumerate(
            (
                probe_real * patch_real - probe_imag * patch_imag,
                probe_real * patch_imag + probe_imag * patch_real,
            )
        ):
            left[0, at, part * width : (part + 1) * width], left[1, at, part * width : (part + 1) * width] = halves(wave)
    inner = product((left[0], left[1]), (table[0], table[1]))
    for slot in range(slots):
        here = inner[slot * width : (slot + 1) * width]
        for part in range(2):
            at = slice(part * width, (part + 1) * width)
            right[0, at, :], right[1, at, :] = halves(here[:, at])
        far_field = product((table_t[0], table_t[1]), (right[0], right[1]))
        far_real, far_imag = far_field[:width], far_field[width:]
        inverse = jnp.minimum(
            lax.rsqrt(far_real * far_real + far_imag * far_imag), 1.0 / modulus_floor
        )
        factor = magnitudes[slot] * inverse - 1.0
        at = slice(slot * width, (slot + 1) * width)
        left[0, at, :width], left[1, at, :width] = halves(far_real * factor)
        left[0, at, width:], left[1, at, width:] = halves(far_imag * factor)
    inner = product((left[0], left[1]), (table_t[0], table_t[1]))
    ext[...] = jnp.zeros_like(ext)
    sums = [jnp.zeros((width, width), jnp.float32)] * 3
    for slot in range(slots):
        here = inner[slot * width : (slot + 1) * width]
        for part in range(2):
            at = slice(part * width, (part + 1) * width)
            right[0, at, :], right[1, at, :] = halves(here[:, at])
        live = jnp.where(slot < live_count, 1.0, 0.0)
        delta = product((table[0], table[1]), (right[0], right[1])) * live
        real, imag = delta[:width], delta[width:]
        patch_real, patch_imag = patches[slot, 0], patches[slot, 1]
        sums = [
            sums[0] + (patch_real * real + patch_imag * imag),
            sums[1] + (patch_real * imag - patch_imag * real),
            sums[2] + live * (patch_real * patch_real + patch_imag * patch_imag),
        ]
        block, row_shift, lane_shift = places[slot]
        for part, grad in enumerate(
            (probe_real * real + probe_imag * imag, probe_real * imag - probe_imag * real)
        ):
            ext[part, *block] += spread(grad, row_shift, lane_shift)
    for layer in range(3):
        for side in range(width // LANES):
            terms[side, layer] = sums[layer][:, side * LANES : (side + 1) * LANES]
    total[...] = jnp.full(total.shape, jnp.sum(sums[2]))
    above[...] = ext[:, :half, :]
    center[...] = ext[:, half : half + tile_r, :]
    below[...] = ext[:, half + tile_r : 2 * half + tile_r, :]


def update(offsets, counts, probe, magnitudes, own, rim, near, near_rim, far, far_rim):
    slots, width = magnitudes.shape[:2]
    half = width // 2
    tile_r, tile_c = own.shape[1:]
    table, table_t = dft_tables(width)
    smem = pl.BlockSpec(memory_space=pltpu.SMEM)
    vmem = pl.BlockSpec(memory_space=pltpu.VMEM)
    strip = jax.ShapeDtypeStruct((2, tile_r, tile_c + 2 * half), jnp.float32)
    return pl.pallas_call(
        update_kernel,
        out_shape=[
            jax.ShapeDtypeStruct((width // LANES, 3, width, LANES), jnp.float32),
            jax.ShapeDtypeStruct((8, LANES), jnp.float32),
            strip,
            strip,
            strip,
        ],
        in_specs=[smem, smem] + [vmem] * 10,
        out_specs=[vmem] * 5,
        scratch_shapes=[
            pltpu.VMEM((2, tile_r + 2 * half + SUBLANES, tile_c + 2 * half), jnp.float32),
            pltpu.VMEM((slots, 2, width, width), jnp.float32),
            pltpu.VMEM((2, slots * width, 2 * width), jnp.bfloat16),
            pltpu.VMEM((2, 2 * width, width), jnp.bfloat16),
        ],
        compiler_params=pltpu.CompilerParams(vmem_limit_bytes=VMEM_LIMIT),
        cost_estimate=pl.CostEstimate(
            flops=3200000000, bytes_accessed=8000000, transcendentals=131072
        ),
    )(offsets, counts, probe, magnitudes, table, table_t, own, rim, near, near_rim, far, far_rim)


def exchange(value, axis, count, bit):
    return lax.ppermute(value, axis, [(i, i ^ bit) for i in range(count)])


def shards(specimen, probe_field, scan_offsets, live_counts, magnitudes):
    rows, cols = lax.axis_size("row"), lax.axis_size("col")
    width = probe_field.shape[1]
    half = width // 2
    tile_r, tile_c = specimen.shape[1:]
    row_place = lax.axis_index("row")
    col_place = lax.axis_index("col")
    row_odd = row_place % 2
    col_odd = col_place % 2
    pairs = [(i, i ^ 1) for i in range(cols)]
    others = [(i, i + 1) for i in range(1, cols - 1, 2)] + [(i + 1, i) for i in range(1, cols - 1, 2)]
    toward = [(i, i + 2) for i in range(1, rows - 2, 2)] + [(i, i - 2) for i in range(2, rows, 2)]
    onward = [(i, i + 2) for i in range(0, rows - 2, 2)] + [(i, i - 2) for i in range(3, rows, 2)]

    low, high = specimen[:, :, :half], specimen[:, :, tile_c - half :]
    pair_rim = lax.ppermute(jnp.where(col_odd == 0, high, low), "col", pairs)
    other_rim = lax.ppermute(jnp.where(col_odd == 0, low, high), "col", others)
    beyond = lax.ppermute(specimen, "row", toward)
    rim = jnp.stack([pair_rim, other_rim])
    beyond_rim = lax.ppermute(rim, "row", toward)
    near = exchange(specimen, "row", rows, 1)
    near_rim = exchange(rim, "row", rows, 1)
    far = exchange(beyond, "row", rows, 1)
    far_rim = exchange(beyond_rim, "row", rows, 1)

    light = lighting(scan_offsets, live_counts, probe_field, tile_r, tile_c)
    terms, total, above, center, below = update(
        scan_offsets, live_counts, probe_field, magnitudes[0, 0],
        specimen, rim, near, near_rim, far, far_rim,
    )

    got_above = exchange(above, "row", rows, 1)
    got_below = exchange(below, "row", rows, 1)
    forward = jnp.where(row_odd == 0, got_below, got_above)
    beyond = lax.ppermute(forward, "row", onward)
    summed = center + jnp.where(row_odd == 0, got_above, got_below) + beyond
    low, high = summed[:, :, :half], summed[:, :, tile_c + half :]
    pair_part = lax.ppermute(jnp.where(col_odd == 0, high, low), "col", pairs)
    other_part = lax.ppermute(jnp.where(col_odd == 0, low, high), "col", others)
    low_part = jnp.where(col_odd == 0, other_part, pair_part)
    high_part = jnp.where(col_odd == 0, pair_part, other_part)
    middle = summed[:, :, half : half + tile_c]
    middle = middle + jnp.concatenate([low_part, high_part], 2)
    specimen_next = specimen + middle / light

    def send(value, total, axis, pairs_here):
        size = value.shape[0] * value.shape[1]
        flat = jnp.concatenate([value.reshape(size, LANES), total])
        got = lax.ppermute(flat, axis, pairs_here)
        return got[:size].reshape(value.shape), total + got[size:]

    def pick(condition, first, second):
        return jnp.where(condition, first, second)

    steps = [("row", rows, 2), ("col", cols, 1)]
    mine = pick(row_odd == 0, terms[0], terms[1])
    given = pick(row_odd == 0, terms[1], terms[0])
    got, total = send(given, total, "row", [(i, i ^ 1) for i in range(rows)])
    value = mine + got
    for axis, count, bit in steps:
        place = (lax.axis_index(axis) // bit) % 2
        size = value.shape[1] // 2
        first, second = value[:, :size], value[:, size:]
        got, total = send(
            pick(place == 0, second, first), total, axis, [(i, i ^ bit) for i in range(count)]
        )
        value = pick(place == 0, first, second) + got
    for bit in (1 << k for k in range(2, rows.bit_length() - 1)):
        got, total = send(value, total, "row", [(i, i ^ bit) for i in range(rows)])
        value = value + got
    line = cols // 2
    chain = line == 4
    if chain:
        around = [(i, i ^ 2) for i in range(cols)]
        got, total = send(value, total, "col", around)
        value = value + got
        across = [(i, (i ^ 6)) for i in range(cols) if (i // 2) in (1, 2)]
        got, total = send(value, total, "col", across)
        value = value + got
    else:
        for bit in (1 << k for k in range(1, cols.bit_length() - 1)):
            got, total = send(value, total, "col", [(i, i ^ bit) for i in range(cols)])
            value = value + got
    size = value.shape[1]
    first_row = (
        ((row_place // 2) % 2) * (width // 2) + col_odd * (width // 4)
    )
    mean = total[0, 0] / (width * width)
    sides = probe_field.reshape(2, width, width // LANES, LANES)
    own_probe = pick(row_odd == 0, sides[:, :, 0], sides[:, :, 1])
    own_probe = lax.dynamic_slice(own_probe, (0, first_row, 0), (2, size, LANES))
    fresh = own_probe + value[:2] / (value[2] + probe_damping * mean)
    if chain:
        inner = ((col_place // 2) == 1) | ((col_place // 2) == 2)
        outward = [(i, i ^ 2) for i in range(cols) if (i // 2) in (1, 2)]
        got = lax.ppermute(fresh, "col", outward)
        fresh = pick(inner, fresh, got)
    for axis, count, bit in reversed(steps):
        place = (lax.axis_index(axis) // bit) % 2
        got = exchange(fresh, axis, count, bit)
        fresh = pick(
            place == 0, jnp.concatenate([fresh, got], 1), jnp.concatenate([got, fresh], 1)
        )
    got = exchange(fresh, "row", rows, 1)
    probe_next = pick(
        row_odd == 0, jnp.concatenate([fresh, got], 2), jnp.concatenate([got, fresh], 2)
    )
    return (specimen_next, probe_next)


def solution(mesh):
    return jax.shard_map(
        shards,
        mesh=mesh,
        in_specs=(P(None, "row", "col"), P(), P(), P(), P("row", "col", None, None, None)),
        out_specs=(P(None, "row", "col"), P()),
        check_vma=False,
    )
```

```python
import functools
import math

import jax
import jax.numpy as jnp
import ml_dtypes
import numpy as np
from jax import lax
from jax.experimental import pallas as pl
from jax.experimental.pallas import tpu as pltpu
from jax.sharding import PartitionSpec as P

modulus_floor = 0.25
object_damping = 0.1
probe_damping = 0.1
LANES = 128
SUBLANES = 8
VMEM_LIMIT = 20 * 1024 * 1024


def dft_table(width):
    counter = np.arange(width)
    angle = (counter[:, None] * counter[None, :] % width) * (2.0 * math.pi / width)
    table = np.concatenate([np.cos(angle), np.sin(angle)], 1) / math.sqrt(width)
    high = table.astype(ml_dtypes.bfloat16)
    low = (table - high.astype(np.float64)).astype(ml_dtypes.bfloat16)
    return np.stack([high, low])


def halves(value):
    high = value.astype(jnp.bfloat16)
    return high, (value - high.astype(jnp.float32)).astype(jnp.bfloat16)


def product(left, right):
    dot = functools.partial(jnp.dot, preferred_element_type=jnp.float32)
    return dot(left[0], right[0]) + (dot(left[1], right[0]) + dot(left[0], right[1]))


def turn(first, second, third, ref, at):
    for place, block in zip(at, (first, second, third)):
        for half_at, half in enumerate(halves(block)):
            ref[half_at, *place] = half


def split_start(start, step, last):
    aligned = jnp.minimum(start // step, last // step) * step
    return pl.multiple_of(aligned, step), start - aligned


def lane_groups(value):
    return [value[..., at : at + LANES] for at in range(0, value.shape[-1], LANES)]


def cut(value, row_shift, lane_shift):
    rows, lanes = value.shape
    value = value.reshape(rows // SUBLANES, SUBLANES, lanes)
    lane_turn = lax.rem(LANES - lane_shift, LANES)
    row_turn = lax.rem(SUBLANES - row_shift, SUBLANES)
    shape = (rows // SUBLANES, SUBLANES, LANES)
    keep_lane = lax.broadcasted_iota(jnp.int32, shape, 2) < LANES - lane_shift
    keep_row = lax.broadcasted_iota(jnp.int32, shape, 1)[1:] < SUBLANES - row_shift
    turned = [pltpu.roll(group, lane_turn, 2) for group in lane_groups(value)]
    parts = []
    for first, second in zip(turned[:-1], turned[1:]):
        part = pltpu.roll(jnp.where(keep_lane, first, second), row_turn, 1)
        part = jnp.where(keep_row, part[:-1], part[1:])
        parts.append(part.reshape(rows - SUBLANES, LANES))
    return jnp.concatenate(parts, 1)


def spread(value, row_shift, lane_shift):
    rows, lanes = value.shape
    value = value.reshape(rows // SUBLANES, SUBLANES, lanes)
    shape = (rows // SUBLANES + 1, SUBLANES, LANES)
    lane_turn = lax.rem(lane_shift, LANES)
    take_lane = lax.broadcasted_iota(jnp.int32, shape, 2) < lane_shift
    take_row = lax.broadcasted_iota(jnp.int32, shape, 1) < row_shift
    blank_row = jnp.zeros((1, SUBLANES, LANES), value.dtype)
    turned = []
    for group in lane_groups(value):
        group = pltpu.roll(group, row_shift, 1)
        group = jnp.where(
            take_row,
            jnp.concatenate([blank_row, group], 0),
            jnp.concatenate([group, blank_row], 0),
        )
        turned.append(pltpu.roll(group, lane_turn, 2))
    blank = jnp.zeros(shape, value.dtype)
    parts = [
        jnp.where(take_lane, first, second).reshape(rows + SUBLANES, LANES)
        for first, second in zip([blank] + turned, turned + [blank])
    ]
    return jnp.concatenate(parts, 1)


def lighting_kernel(offsets, counts, probe, out, pad):
    rows, cols, slots = offsets.shape[:3]
    tile_r, tile_c = out.shape
    width = probe.shape[1]
    half = width // 2
    row_place = lax.axis_index("row")
    col_place = lax.axis_index("col")
    power = probe[0] * probe[0] + probe[1] * probe[1]
    pad[...] = jnp.zeros_like(pad)
    pad[tile_r : tile_r + width, tile_c : tile_c + width] = power
    out[...] = jnp.full(out.shape, object_damping * jnp.max(power))
    wide = tile_c + LANES
    for row_step in (-1, 0, 1):
        for col_step in (-1, 0, 1):
            row, col = row_place + row_step, col_place + col_step
            inside = (row >= 0) & (row < rows) & (col >= 0) & (col < cols)
            row_at = jnp.clip(row, 0, rows - 1)
            col_at = jnp.clip(col, 0, cols - 1)
            for slot in range(slots):
                top = offsets[row_at, col_at, slot, 0] + row_step * tile_r
                left = offsets[row_at, col_at, slot, 1] + col_step * tile_c

                @pl.when(
                    inside
                    & (slot < counts[row_at, col_at])
                    & (left > -width)
                    & (left < tile_c)
                )
                def _():
                    row, row_shift = split_start(tile_r - top, SUBLANES, tile_r + width)
                    lane, lane_shift = split_start(tile_c - left, LANES, pad.shape[1] - wide)
                    part = pad[pl.ds(row, tile_r + SUBLANES), pl.ds(lane, wide)]
                    out[...] += cut(part, row_shift, lane_shift)


def lighting(offsets, counts, probe, tile_r, tile_c):
    width = probe.shape[1]
    smem = pl.BlockSpec(memory_space=pltpu.SMEM)
    vmem = pl.BlockSpec(memory_space=pltpu.VMEM)
    return pl.pallas_call(
        lighting_kernel,
        out_shape=jax.ShapeDtypeStruct((tile_r, tile_c), jnp.float32),
        in_specs=[smem, smem, vmem],
        out_specs=vmem,
        scratch_shapes=[
            pltpu.VMEM((2 * tile_r + width + SUBLANES, 2 * tile_c + width), jnp.float32)
        ],
        compiler_params=pltpu.CompilerParams(vmem_limit_bytes=VMEM_LIMIT),
        cost_estimate=pl.CostEstimate(flops=4000000, bytes_accessed=800000, transcendentals=0),
    )(offsets, counts, probe)


def patch_block(offsets, row_place, col_place, slot, half, tile_r, width):
    row, row_shift = split_start(offsets[row_place, col_place, slot, 0] + half, SUBLANES, tile_r)
    lane, lane_shift = split_start(
        offsets[row_place, col_place, slot, 1] + half, LANES, 2 * half - LANES
    )
    return (pl.ds(row, width + SUBLANES), pl.ds(lane, width + LANES)), row_shift, lane_shift


def delta_kernel(
    offsets, counts, probe, magnitudes, table, own, rim, near, near_rim, far, far_rim,
    kept, given, own_probe, delta, ext, patches, left, right, stack, basis_in, measured, arrived,
):
    table_copy = pltpu.make_async_copy(table, basis_in, arrived.at[0])
    measured_copy = pltpu.make_async_copy(magnitudes, measured, arrived.at[1])
    table_copy.start()
    measured_copy.start()
    slots, width = magnitudes.shape[0], magnitudes.shape[1]
    half = width // 2
    tile_r, tile_c = own.shape[1:]
    row_place = lax.axis_index("row")
    col_place = lax.axis_index("col")
    row_odd = lax.rem(row_place, 2)
    col_odd = lax.rem(col_place, 2)
    near_row = pl.multiple_of((1 - row_odd) * (tile_r + half), half)
    far_row = pl.multiple_of(row_odd * (tile_r + half), half)
    pair_col = pl.multiple_of((1 - col_odd) * (tile_c + half), half)
    other_col = pl.multiple_of(col_odd * (tile_c + half), half)
    far_at = row_place + 2 * row_odd - 1
    inside = (far_at >= 0) & (far_at < lax.axis_size("row"))
    for part in range(2):
        for rows, mid, edge in ((half, own, rim), (near_row, near, near_rim)):
            at = pl.ds(rows, tile_r)
            ext[part, at, half : half + tile_c] = mid[part]
            ext[part, at, pl.ds(pair_col, half)] = edge[0, part]
            ext[part, at, pl.ds(other_col, half)] = edge[1, part]
        at = pl.ds(far_row, tile_r)
        ext[part, at, half : half + tile_c] = jnp.where(inside, far[part], 0.0)
        ext[part, at, pl.ds(pair_col, half)] = jnp.where(inside, far_rim[0, part], 0.0)
        ext[part, at, pl.ds(other_col, half)] = jnp.where(inside, far_rim[1, part], 0.0)
    live_count = counts[row_place, col_place]
    probe_real, probe_imag = probe[0], probe[1]
    first = slice(0, 2 * width)
    second = slice(width, 3 * width)
    places = [slice(k * width, (k + 1) * width) for k in range(3)]
    for slot in range(slots):
        block, row_shift, lane_shift = patch_block(
            offsets, row_place, col_place, slot, half, tile_r, width
        )
        for part in range(2):
            patches[slot, part] = cut(ext[part, *block], row_shift, lane_shift)
        patch_real, patch_imag = patches[slot, 0], patches[slot, 1]
        real = probe_real * patch_real - probe_imag * patch_imag
        imag = probe_real * patch_imag + probe_imag * patch_real
        at = slice(slot * width, (slot + 1) * width)
        turn(real, imag, -real, left, [(at, place) for place in places])
    table_copy.wait()
    stack[:, :width] = basis_in[:, :, :width]
    stack[:, width:] = basis_in[:, :, width:]
    basis = (stack[0], stack[1])
    basis_left = (basis_in[0], basis_in[1])
    real = product((left[0, :, first], left[1, :, first]), basis)
    imag = product((left[0, :, second], left[1, :, second]), basis)
    measured_copy.wait()
    for slot in range(slots):
        at = slice(slot * width, (slot + 1) * width)
        turn(real[at], imag[at], -real[at], right, [(place,) for place in places])
        far_real = product(basis_left, (right[0, first], right[1, first]))
        far_imag = product(basis_left, (right[0, second], right[1, second]))
        inverse = jnp.minimum(
            lax.rsqrt(far_real * far_real + far_imag * far_imag), 1.0 / modulus_floor
        )
        factor = measured[slot] * inverse - 1.0
        back_real, back_imag = far_real * factor, far_imag * factor
        turn(back_imag, back_real, -back_imag, left, [(at, place) for place in places])
    imag = product((left[0, :, first], left[1, :, first]), basis)
    real = product((left[0, :, second], left[1, :, second]), basis)
    sums = [jnp.zeros((width, width), jnp.float32)] * 3
    for slot in range(slots):
        at = slice(slot * width, (slot + 1) * width)
        turn(imag[at], real[at], -imag[at], right, [(place,) for place in places])
        live = jnp.where(slot < live_count, 1.0, 0.0)
        delta_imag = product(basis_left, (right[0, first], right[1, first])) * live
        delta_real = product(basis_left, (right[0, second], right[1, second])) * live
        delta[slot, 0] = delta_real
        delta[slot, 1] = delta_imag
        patch_real, patch_imag = patches[slot, 0], patches[slot, 1]
        sums = [
            sums[0] + (patch_real * delta_real + patch_imag * delta_imag),
            sums[1] + (patch_real * delta_imag - patch_imag * delta_real),
            sums[2] + live * (patch_real * patch_real + patch_imag * patch_imag),
        ]
    even = row_odd == 0
    for layer in range(3):
        low, high = lane_groups(sums[layer])
        kept[layer * width : (layer + 1) * width] = jnp.where(even, low, high)
        given[layer * width : (layer + 1) * width] = jnp.where(even, high, low)
    total = jnp.full((SUBLANES, LANES), jnp.sum(sums[2]))
    kept[3 * width :] = total
    given[3 * width :] = total
    size = own_probe.shape[1]
    row = pl.multiple_of(lax.rem(row_place // 2, 2) * (2 * size) + col_odd * size, size)
    for part in range(2):
        low, high = lane_groups(probe[part, pl.ds(row, size), :])
        own_probe[part] = jnp.where(even, low, high)


def place_kernel(
    offsets, probe, delta, center, close, onward, center_rim, close_rim, onward_rim, ext
):
    slots, width = delta.shape[0], delta.shape[2]
    half = width // 2
    tile_r, tile_c = center.shape[1:]
    row_place = lax.axis_index("row")
    col_place = lax.axis_index("col")
    row_odd = lax.rem(row_place, 2)
    col_odd = lax.rem(col_place, 2)
    ext[...] = jnp.zeros_like(ext)
    probe_real, probe_imag = probe[0], probe[1]
    for slot in range(slots):
        real, imag = delta[slot, 0], delta[slot, 1]
        block, row_shift, lane_shift = patch_block(
            offsets, row_place, col_place, slot, half, tile_r, width
        )
        for part, grad in enumerate(
            (probe_real * real + probe_imag * imag, probe_real * imag - probe_imag * real)
        ):
            ext[part, *block] += spread(grad, row_shift, lane_shift)
    near_row = pl.multiple_of((1 - row_odd) * (tile_r + half), half)
    far_row = pl.multiple_of(row_odd * (tile_r + half), half)
    pair_col = pl.multiple_of((1 - col_odd) * (tile_c + half), half)
    other_col = pl.multiple_of(col_odd * (tile_c + half), half)
    for row, mid, rim in (
        (half, center, center_rim),
        (near_row, close, close_rim),
        (far_row, onward, onward_rim),
    ):
        at = pl.ds(row, tile_r)
        mid[...] = ext[:, at, half : half + tile_c]
        rim[0] = ext[:, at, pl.ds(pair_col, half)]
        rim[1] = ext[:, at, pl.ds(other_col, half)]


def exit_update(offsets, counts, probe, magnitudes, own, rim, near, near_rim, far, far_rim):
    slots, width = magnitudes.shape[:2]
    half = width // 2
    tile_r, tile_c = own.shape[1:]
    smem = pl.BlockSpec(memory_space=pltpu.SMEM)
    vmem = pl.BlockSpec(memory_space=pltpu.VMEM)
    return pl.pallas_call(
        delta_kernel,
        out_shape=[
            jax.ShapeDtypeStruct((3 * width + SUBLANES, LANES), jnp.float32),
            jax.ShapeDtypeStruct((3 * width + SUBLANES, LANES), jnp.float32),
            jax.ShapeDtypeStruct((2, width // 4, LANES), jnp.float32),
            jax.ShapeDtypeStruct((slots, 2, width, width), jnp.float32),
        ],
        in_specs=[smem, smem, vmem] + [pl.BlockSpec(memory_space=pltpu.HBM)] * 2 + [vmem] * 6,
        out_specs=[vmem] * 4,
        scratch_shapes=[
            pltpu.VMEM((2, tile_r + 2 * half + SUBLANES, tile_c + 2 * half), jnp.float32),
            pltpu.VMEM((slots, 2, width, width), jnp.float32),
            pltpu.VMEM((2, slots * width, 3 * width), jnp.bfloat16),
            pltpu.VMEM((2, 3 * width, width), jnp.bfloat16),
            pltpu.VMEM((2, 2 * width, width), jnp.bfloat16),
            pltpu.VMEM((2, width, 2 * width), jnp.bfloat16),
            pltpu.VMEM((slots, width, width), jnp.float32),
            pltpu.SemaphoreType.DMA((2,)),
        ],
        compiler_params=pltpu.CompilerParams(vmem_limit_bytes=VMEM_LIMIT),
        cost_estimate=pl.CostEstimate(
            flops=3200000000, bytes_accessed=8000000, transcendentals=131072
        ),
    )(
        offsets, counts, probe, in_hbm(magnitudes), in_hbm(jnp.asarray(dft_table(width))),
        *map(in_vmem, (own, rim, near, near_rim, far, far_rim)),
    )


def in_hbm(value):
    return pltpu.with_memory_space_constraint(value, pltpu.HBM)


def in_vmem(value):
    return pltpu.with_memory_space_constraint(value, pltpu.VMEM)


def fold_kernel(axis, bit, kept_in, got, kept, given):
    layers = 3
    size = (kept.shape[0] - SUBLANES) // layers
    odd = lax.rem(lax.axis_index(axis) // bit, 2)
    for layer in range(layers):
        first = 2 * layer * size
        mine = pl.ds(pl.multiple_of(first + odd * size, SUBLANES), size)
        other = pl.ds(pl.multiple_of(first + (1 - odd) * size, SUBLANES), size)
        at = slice(layer * size, (layer + 1) * size)
        kept[at] = kept_in[mine] + got[mine]
        given[at] = kept_in[other] + got[other]
    total = kept_in[2 * layers * size :] + got[2 * layers * size :]
    kept[layers * size :] = total
    given[layers * size :] = total


def fold(kept, got, axis, bit):
    vmem = pl.BlockSpec(memory_space=pltpu.VMEM)
    shape = jax.ShapeDtypeStruct(((kept.shape[0] + SUBLANES) // 2, LANES), jnp.float32)
    return pl.pallas_call(
        functools.partial(fold_kernel, axis, bit),
        out_shape=[shape] * 2,
        in_specs=[vmem] * 2,
        out_specs=[vmem] * 2,
        compiler_params=pltpu.CompilerParams(vmem_limit_bytes=VMEM_LIMIT),
        cost_estimate=pl.CostEstimate(flops=100000, bytes_accessed=400000, transcendentals=0),
    )(in_vmem(kept), in_vmem(got))


def place(offsets, probe, delta, tile_r, tile_c):
    width = probe.shape[1]
    half = width // 2
    smem = pl.BlockSpec(memory_space=pltpu.SMEM)
    vmem = pl.BlockSpec(memory_space=pltpu.VMEM)
    middle = jax.ShapeDtypeStruct((2, tile_r, tile_c), jnp.float32)
    rim = jax.ShapeDtypeStruct((2, 2, tile_r, half), jnp.float32)
    return pl.pallas_call(
        place_kernel,
        out_shape=[middle] * 3 + [rim] * 3,
        in_specs=[smem, vmem, vmem],
        out_specs=[vmem] * 6,
        scratch_shapes=[
            pltpu.VMEM((2, tile_r + 2 * half + SUBLANES, tile_c + 2 * half), jnp.float32),
        ],
        compiler_params=pltpu.CompilerParams(vmem_limit_bytes=VMEM_LIMIT),
        cost_estimate=pl.CostEstimate(flops=4000000, bytes_accessed=4000000, transcendentals=0),
    )(offsets, probe, delta)


def exchange(value, axis, count, bit):
    return lax.ppermute(value, axis, [(i, i ^ bit) for i in range(count)])


def shards(specimen, probe_field, scan_offsets, live_counts, magnitudes):
    rows, cols = lax.axis_size("row"), lax.axis_size("col")
    width = probe_field.shape[1]
    half = width // 2
    tile_r, tile_c = specimen.shape[1:]
    row_place = lax.axis_index("row")
    col_place = lax.axis_index("col")
    row_odd = row_place % 2
    col_odd = col_place % 2
    pairs = [(i, i ^ 1) for i in range(cols)]
    others = [(i, i + 1) for i in range(1, cols - 1, 2)] + [(i + 1, i) for i in range(1, cols - 1, 2)]
    toward = [(i, i + 2) for i in range(1, rows - 2, 2)] + [(i, i - 2) for i in range(2, rows, 2)]
    toward += [(rows - 1, rows - 2), (0, 1)]
    onward_pairs = [(target, source) for source, target in toward]

    low, high = specimen[:, :, :half], specimen[:, :, tile_c - half :]
    pair_rim = lax.ppermute(jnp.where(col_odd == 0, high, low), "col", pairs)
    other_rim = lax.ppermute(jnp.where(col_odd == 0, low, high), "col", others)
    beyond = lax.ppermute(specimen, "row", toward)
    rim = jnp.stack([pair_rim, other_rim])
    beyond_rim = lax.ppermute(rim, "row", toward)
    near = exchange(specimen, "row", rows, 1)
    near_rim = exchange(rim, "row", rows, 1)
    far = exchange(beyond, "row", rows, 1)
    far_rim = exchange(beyond_rim, "row", rows, 1)

    kept, given, own_probe, delta = exit_update(
        scan_offsets, live_counts, probe_field, magnitudes[0, 0],
        specimen, rim, near, near_rim, far, far_rim,
    )

    def pick(condition, first, second):
        return jnp.where(condition, first, second)

    def join(value, axis, count, bit):
        place_here = (lax.axis_index(axis) // bit) % 2
        got = exchange(value, axis, count, bit)
        return pick(
            place_here == 0,
            jnp.concatenate([value, got], 1),
            jnp.concatenate([got, value], 1),
        )

    tie = lax.optimization_barrier
    got = exchange(given, "row", rows, 1)
    center, close, onward, center_rim, close_rim, onward_rim = place(
        scan_offsets, probe_field, delta, tile_r, tile_c
    )
    got, close, onward, close_rim, onward_rim = tie((got, close, onward, close_rim, onward_rim))
    kept, given = fold(kept, got, "row", 2)
    got_close_rim = exchange(close_rim, "row", rows, 1)
    got_onward_rim = exchange(onward_rim, "row", rows, 1)
    got_close = exchange(close, "row", rows, 1)
    got_onward = exchange(onward, "row", rows, 1)
    probe_late, given = tie((probe_field, given))
    light = lighting(scan_offsets, live_counts, probe_late, tile_r, tile_c)
    got = exchange(given, "row", rows, 2)
    got, got_onward_rim, got_onward, light = tie((got, got_onward_rim, got_onward, light))
    kept, given = fold(kept, got, "col", 1)
    value = kept + exchange(given, "col", cols, 1)
    value, got_onward_rim, got_onward = tie((value, got_onward_rim, got_onward))
    beyond_rim = lax.ppermute(got_onward_rim, "row", onward_pairs)
    beyond = lax.ppermute(got_onward, "row", onward_pairs)
    for bit in (1 << k for k in range(1, cols.bit_length() - 1)):
        value = value + exchange(value, "col", cols, 2 * bit - 2)
    for bit in (1 << k for k in range(2, rows.bit_length() - 1)):
        value = value + exchange(value, "row", rows, bit)
    value, beyond_rim = tie((value, beyond_rim))
    inside = (row_place + 2 * row_odd - 1 >= 0) & (row_place + 2 * row_odd - 1 < rows)
    rim_sum = center_rim + got_close_rim + pick(inside, beyond_rim, 0.0)
    pair_part = lax.ppermute(rim_sum[0], "col", pairs)
    other_part = lax.ppermute(rim_sum[1], "col", others)
    size = own_probe.shape[1]
    real, imag, weight, total = (value[k * size : (k + 1) * size] for k in range(4))
    update = jnp.stack([real, imag]) / (weight + probe_damping * (total[:1] / (width * width)))
    fresh = own_probe + update
    fresh = join(fresh, "col", cols, 1)
    fresh, pair_part = tie((fresh, pair_part))
    fresh = join(fresh, "row", rows, 2)
    fresh, other_part, beyond = tie((fresh, other_part, beyond))
    got = exchange(fresh, "row", rows, 1)
    low_part = pick(col_odd == 0, other_part, pair_part)
    high_part = pick(col_odd == 0, pair_part, other_part)
    middle = center + got_close + pick(inside, beyond, 0.0)
    middle = middle + jnp.concatenate([low_part, high_part], 2)
    specimen_next = specimen + middle / light
    probe_next = pick(
        row_odd == 0, jnp.concatenate([fresh, got], 2), jnp.concatenate([got, fresh], 2)
    )
    return (specimen_next, probe_next)


def solution(mesh):
    return jax.shard_map(
        shards,
        mesh=mesh,
        in_specs=(P(None, "row", "col"), P(), P(), P(), P("row", "col", None, None, None)),
        out_specs=(P(None, "row", "col"), P()),
        check_vma=False,
    )
```

```python
import functools
import math

import jax
import jax.numpy as jnp
import ml_dtypes
import numpy as np
from jax import lax
from jax.experimental import pallas as pl
from jax.experimental.pallas import tpu as pltpu
from jax.sharding import PartitionSpec as P

modulus_floor = 0.25
object_damping = 0.1
probe_damping = 0.1
LANES = 128
SUBLANES = 8
VMEM_LIMIT = 20 * 1024 * 1024


def dft_tables(width):
    half = width // 2
    counter = np.arange(half)
    tables = []
    for odd in range(2):
        phase = counter[:, None] * (2 * counter[None, :] + odd) % width
        angle = phase * (2.0 * math.pi / width)
        real, imag = np.cos(angle) / math.sqrt(width), -np.sin(angle) / math.sqrt(width)
        tables.append(np.block([[real, imag], [-imag, real]]))
    tables = np.stack(tables + [table.T for table in tables])
    high = tables.astype(ml_dtypes.bfloat16)
    low = (tables - high.astype(np.float64)).astype(ml_dtypes.bfloat16)
    return np.stack([high, low], 1)


def halves(value):
    high = value.astype(jnp.bfloat16)
    return high, (value - high.astype(jnp.float32)).astype(jnp.bfloat16)


def product(left, right):
    dot = functools.partial(jnp.dot, preferred_element_type=jnp.float32)
    return dot(left[0], right[0]) + (dot(left[1], right[0]) + dot(left[0], right[1]))


def keep(ref, rows, lanes, value):
    for place, half in enumerate(halves(value)):
        ref[place, rows, lanes] = half


def product_of(left, right):
    return product((left[0], left[1]), (right[0], right[1]))


def split_start(start, step, last):
    aligned = jnp.minimum(start // step, last // step) * step
    return pl.multiple_of(aligned, step), start - aligned


def lane_groups(value):
    return [value[..., at : at + LANES] for at in range(0, value.shape[-1], LANES)]


def cut(value, row_shift, lane_shift):
    rows, lanes = value.shape
    value = value.reshape(rows // SUBLANES, SUBLANES, lanes)
    lane_turn = lax.rem(LANES - lane_shift, LANES)
    row_turn = lax.rem(SUBLANES - row_shift, SUBLANES)
    shape = (rows // SUBLANES, SUBLANES, LANES)
    keep_lane = lax.broadcasted_iota(jnp.int32, shape, 2) < LANES - lane_shift
    keep_row = lax.broadcasted_iota(jnp.int32, shape, 1)[1:] < SUBLANES - row_shift
    turned = [pltpu.roll(group, lane_turn, 2) for group in lane_groups(value)]
    parts = []
    for first, second in zip(turned[:-1], turned[1:]):
        part = pltpu.roll(jnp.where(keep_lane, first, second), row_turn, 1)
        part = jnp.where(keep_row, part[:-1], part[1:])
        parts.append(part.reshape(rows - SUBLANES, LANES))
    return jnp.concatenate(parts, 1)


def spread(value, row_shift, lane_shift):
    rows, lanes = value.shape
    value = value.reshape(rows // SUBLANES, SUBLANES, lanes)
    shape = (rows // SUBLANES + 1, SUBLANES, LANES)
    lane_turn = lax.rem(lane_shift, LANES)
    take_lane = lax.broadcasted_iota(jnp.int32, shape, 2) < lane_shift
    take_row = lax.broadcasted_iota(jnp.int32, shape, 1) < row_shift
    blank_row = jnp.zeros((1, SUBLANES, LANES), value.dtype)
    turned = []
    for group in lane_groups(value):
        group = pltpu.roll(group, row_shift, 1)
        group = jnp.where(
            take_row,
            jnp.concatenate([blank_row, group], 0),
            jnp.concatenate([group, blank_row], 0),
        )
        turned.append(pltpu.roll(group, lane_turn, 2))
    blank = jnp.zeros(shape, value.dtype)
    parts = [
        jnp.where(take_lane, first, second).reshape(rows + SUBLANES, LANES)
        for first, second in zip([blank] + turned, turned + [blank])
    ]
    return jnp.concatenate(parts, 1)


def lighting_kernel(offsets, counts, probe, out, pad):
    rows, cols, slots = offsets.shape[:3]
    tile_r, tile_c = out.shape
    width = probe.shape[1]
    half = width // 2
    row_place = lax.axis_index("row")
    col_place = lax.axis_index("col")
    power = probe[0] * probe[0] + probe[1] * probe[1]
    pad[...] = jnp.zeros_like(pad)
    pad[tile_r : tile_r + width, tile_c : tile_c + width] = power
    out[...] = jnp.full(out.shape, object_damping * jnp.max(power))
    wide = tile_c + LANES
    for row_step in (-1, 0, 1):
        for col_step in (-1, 0, 1):
            row, col = row_place + row_step, col_place + col_step
            inside = (row >= 0) & (row < rows) & (col >= 0) & (col < cols)
            row_at = jnp.clip(row, 0, rows - 1)
            col_at = jnp.clip(col, 0, cols - 1)
            for slot in range(slots):
                top = offsets[row_at, col_at, slot, 0] + row_step * tile_r
                left = offsets[row_at, col_at, slot, 1] + col_step * tile_c

                @pl.when(
                    inside
                    & (slot < counts[row_at, col_at])
                    & (left > -width)
                    & (left < tile_c)
                )
                def _():
                    row, row_shift = split_start(tile_r - top, SUBLANES, tile_r + width)
                    lane, lane_shift = split_start(tile_c - left, LANES, pad.shape[1] - wide)
                    part = pad[pl.ds(row, tile_r + SUBLANES), pl.ds(lane, wide)]
                    out[...] += cut(part, row_shift, lane_shift)


def lighting(offsets, counts, probe, tile_r, tile_c):
    width = probe.shape[1]
    smem = pl.BlockSpec(memory_space=pltpu.SMEM)
    vmem = pl.BlockSpec(memory_space=pltpu.VMEM)
    return pl.pallas_call(
        lighting_kernel,
        out_shape=jax.ShapeDtypeStruct((tile_r, tile_c), jnp.float32),
        in_specs=[smem, smem, vmem],
        out_specs=vmem,
        scratch_shapes=[
            pltpu.VMEM((2 * tile_r + width + SUBLANES, 2 * tile_c + width), jnp.float32)
        ],
        compiler_params=pltpu.CompilerParams(vmem_limit_bytes=VMEM_LIMIT),
        cost_estimate=pl.CostEstimate(flops=40000000, bytes_accessed=8000000, transcendentals=0),
    )(offsets, counts, probe)


def patch_block(offsets, row_place, col_place, slot, half, tile_r, width):
    row, row_shift = split_start(offsets[row_place, col_place, slot, 0] + half, SUBLANES, tile_r)
    lane, lane_shift = split_start(
        offsets[row_place, col_place, slot, 1] + half, LANES, 2 * half - LANES
    )
    return (pl.ds(row, width + SUBLANES), pl.ds(lane, width + LANES)), row_shift, lane_shift


def delta_kernel(
    offsets, counts, probe, magnitudes, tables,
    own, pair_rim, other_rim, near, near_pair, near_other, far, far_pair, far_other,
    kept, given, own_probe, delta, ext, patches, tall_even, tall_odd, wide_even, wide_odd,
):
    slots, width = magnitudes.shape[0], magnitudes.shape[1]
    half = width // 2
    tile_r, tile_c = own.shape[1:]
    row_place = lax.axis_index("row")
    col_place = lax.axis_index("col")
    row_odd = lax.rem(row_place, 2)
    col_odd = lax.rem(col_place, 2)
    near_row = pl.multiple_of((1 - row_odd) * (tile_r + half), half)
    far_row = pl.multiple_of(row_odd * (tile_r + half), half)
    pair_col = pl.multiple_of((1 - col_odd) * (tile_c + half), half)
    other_col = pl.multiple_of(col_odd * (tile_c + half), half)
    far_at = row_place + 2 * row_odd - 1
    inside = (far_at >= 0) & (far_at < lax.axis_size("row"))
    strips = (
        (half, True, own, pair_rim, other_rim),
        (near_row, True, near, near_pair, near_other),
        (far_row, inside, far, far_pair, far_other),
    )
    for part in range(2):
        for row, valid, *blocks in strips:
            at = pl.ds(row, tile_r)
            mid, pair, other = (
                block[part] if valid is True else jnp.where(valid, block[part], 0.0)
                for block in blocks
            )
            ext[part, at, half : half + tile_c] = mid
            ext[part, at, pl.ds(pair_col, half)] = pair
            ext[part, at, pl.ds(other_col, half)] = other
    live_count = counts[row_place, col_place]
    probe_real, probe_imag = probe[0], probe[1]
    right_even, right_odd, left_even, left_odd = (tables.at[k] for k in range(4))
    low, high = slice(0, half), slice(half, width)
    for slot in range(slots):
        block, row_shift, lane_shift = patch_block(
            offsets, row_place, col_place, slot, half, tile_r, width
        )
        for part in range(2):
            patches[slot, part] = cut(ext[part, *block], row_shift, lane_shift)
        patch_real, patch_imag = patches[slot, 0], patches[slot, 1]
        at = slice(slot * width, (slot + 1) * width)
        for part, wave in (
            (low, probe_real * patch_real - probe_imag * patch_imag),
            (high, probe_real * patch_imag + probe_imag * patch_real),
        ):
            keep(tall_even, at, part, wave[:, low] + wave[:, high])
            keep(tall_odd, at, part, wave[:, low] - wave[:, high])
    inner = (product_of(tall_even, right_even), product_of(tall_odd, right_odd))
    for slot in range(slots):
        top = slice(slot * width, slot * width + half)
        bottom = slice(slot * width + half, (slot + 1) * width)
        for odd in range(2):
            at = slice(slot * width + odd * half, slot * width + (odd + 1) * half)
            for part in (low, high):
                upper, lower = inner[odd][top, part], inner[odd][bottom, part]
                keep(wide_even, part, at, upper + lower)
                keep(wide_odd, part, at, upper - lower)
    outer = (product_of(left_even, wide_even), product_of(left_odd, wide_odd))
    for slot in range(slots):
        lanes = slice(slot * width, (slot + 1) * width)
        for odd in range(2):
            far_real, far_imag = outer[odd][low, lanes], outer[odd][high, lanes]
            inverse = jnp.minimum(
                lax.rsqrt(far_real * far_real + far_imag * far_imag), 1.0 / modulus_floor
            )
            factor = magnitudes[slot, odd * half : (odd + 1) * half] * inverse - 1.0
            at = slice(slot * width + odd * half, slot * width + (odd + 1) * half)
            for part, back in ((low, far_real * factor), (high, far_imag * factor)):
                keep(tall_even, at, part, back[:, low])
                keep(tall_odd, at, part, back[:, high])
    inner = (product_of(tall_even, left_even), product_of(tall_odd, left_odd))
    for slot in range(slots):
        for odd, ref in enumerate((wide_even, wide_odd)):
            at = slice(slot * width + odd * half, slot * width + (odd + 1) * half)
            for part in (low, high):
                one, other = inner[0][at, part], inner[1][at, part]
                keep(ref, part, slice(slot * width, slot * width + half), one + other)
                keep(ref, part, slice(slot * width + half, (slot + 1) * width), one - other)
    outer = (product_of(right_even, wide_even), product_of(right_odd, wide_odd))
    sums = [jnp.zeros((width, width), jnp.float32)] * 3
    for slot in range(slots):
        live = jnp.where(slot < live_count, 1.0, 0.0)
        lanes = slice(slot * width, (slot + 1) * width)
        for part, rows in enumerate((low, high)):
            one, other = outer[0][rows, lanes], outer[1][rows, lanes]
            delta[slot, part, low] = (one + other) * live
            delta[slot, part, high] = (one - other) * live
        delta_real, delta_imag = delta[slot, 0], delta[slot, 1]
        patch_real, patch_imag = patches[slot, 0], patches[slot, 1]
        sums = [
            sums[0] + (patch_real * delta_real + patch_imag * delta_imag),
            sums[1] + (patch_real * delta_imag - patch_imag * delta_real),
            sums[2] + live * (patch_real * patch_real + patch_imag * patch_imag),
        ]
    even = row_odd == 0
    for layer in range(3):
        one, other = lane_groups(sums[layer])
        kept[layer * width : (layer + 1) * width] = jnp.where(even, one, other)
        given[layer * width : (layer + 1) * width] = jnp.where(even, other, one)
    total = jnp.full((SUBLANES, LANES), jnp.sum(sums[2]))
    kept[3 * width :] = total
    given[3 * width :] = total
    size = own_probe.shape[1]
    row = pl.multiple_of(lax.rem(row_place // 2, 2) * (2 * size) + col_odd * size, size)
    for part in range(2):
        one, other = lane_groups(probe[part, pl.ds(row, size), :])
        own_probe[part] = jnp.where(even, one, other)


def place_kernel(
    offsets, probe, delta, *blocks_and_ext
):
    *blocks, ext = blocks_and_ext
    slots, width = delta.shape[0], delta.shape[2]
    half = width // 2
    tile_r = blocks[0].shape[1]
    tile_c = ext.shape[2] - 2 * half
    row_place = lax.axis_index("row")
    col_place = lax.axis_index("col")
    row_odd = lax.rem(row_place, 2)
    col_odd = lax.rem(col_place, 2)
    ext[...] = jnp.zeros_like(ext)
    probe_real, probe_imag = probe[0], probe[1]
    for slot in range(slots):
        real, imag = delta[slot, 0], delta[slot, 1]
        block, row_shift, lane_shift = patch_block(
            offsets, row_place, col_place, slot, half, tile_r, width
        )
        for part, grad in enumerate(
            (probe_real * real + probe_imag * imag, probe_real * imag - probe_imag * real)
        ):
            ext[part, *block] += spread(grad, row_shift, lane_shift)
    near_row = pl.multiple_of((1 - row_odd) * (tile_r + half), half)
    far_row = pl.multiple_of(row_odd * (tile_r + half), half)
    pair_col = pl.multiple_of((1 - col_odd) * (tile_c + half), half)
    other_col = pl.multiple_of(col_odd * (tile_c + half), half)
    for k, row in enumerate((half, near_row, far_row)):
        low, high, pair, other = blocks[4 * k : 4 * k + 4]
        at = pl.ds(row, tile_r)
        low[...] = ext[:, at, half : half + tile_c // 2]
        high[...] = ext[:, at, half + tile_c // 2 : half + tile_c]
        pair[...] = ext[:, at, pl.ds(pair_col, half)]
        other[...] = ext[:, at, pl.ds(other_col, half)]


def stage_kernel(magnitudes, tables, ordered, held, measured, arrived):
    slots, width = magnitudes.shape[:2]
    copies = [
        pltpu.make_async_copy(tables, held, arrived.at[0]),
        pltpu.make_async_copy(magnitudes, measured, arrived.at[1]),
    ]
    for copy in copies:
        copy.start()
    line = lax.broadcasted_iota(jnp.int32, (width, width), 0)
    place = lax.broadcasted_iota(jnp.int32, (width, width), 1)

    def chosen(here, there):
        source = jnp.where(here < width // 2, 2 * here, 2 * here - (width - 1))
        return jnp.where(source == there, 1.0, 0.0).astype(jnp.bfloat16)

    by_row, by_lane = chosen(line, place), chosen(place, line)
    copies[1].wait()
    for slot in range(slots):
        rest = measured[slot]
        total = jnp.zeros((width, width), jnp.float32)
        for _ in range(3):
            piece = rest.astype(jnp.bfloat16)
            rest = rest - piece.astype(jnp.float32)
            piece = jnp.dot(by_row, piece, preferred_element_type=jnp.float32)
            total += jnp.dot(
                piece.astype(jnp.bfloat16), by_lane, preferred_element_type=jnp.float32
            )
        ordered[slot] = total
    copies[0].wait()


def stage(magnitudes):
    width = magnitudes.shape[-1]
    hbm = pl.BlockSpec(memory_space=pltpu.HBM)
    vmem = pl.BlockSpec(memory_space=pltpu.VMEM)
    return pl.pallas_call(
        stage_kernel,
        out_shape=[
            jax.ShapeDtypeStruct(magnitudes.shape, jnp.float32),
            jax.ShapeDtypeStruct((4, 2, width, width), jnp.bfloat16),
        ],
        in_specs=[hbm] * 2,
        out_specs=[vmem] * 2,
        scratch_shapes=[
            pltpu.VMEM(magnitudes.shape, jnp.float32),
            pltpu.SemaphoreType.DMA((2,)),
        ],
        compiler_params=pltpu.CompilerParams(vmem_limit_bytes=VMEM_LIMIT),
        cost_estimate=pl.CostEstimate(flops=400000000, bytes_accessed=3000000, transcendentals=0),
    )(in_hbm(magnitudes), in_hbm(jnp.asarray(dft_tables(width))))


def exit_update(offsets, counts, probe, staged, blocks):
    slots, width = staged[0].shape[:2]
    own = blocks[0]
    half = width // 2
    tile_r, tile_c = own.shape[1:]
    smem = pl.BlockSpec(memory_space=pltpu.SMEM)
    vmem = pl.BlockSpec(memory_space=pltpu.VMEM)
    return pl.pallas_call(
        delta_kernel,
        out_shape=[
            jax.ShapeDtypeStruct((3 * width + SUBLANES, LANES), jnp.float32),
            jax.ShapeDtypeStruct((3 * width + SUBLANES, LANES), jnp.float32),
            jax.ShapeDtypeStruct((2, width // 4, LANES), jnp.float32),
            jax.ShapeDtypeStruct((slots, 2, width, width), jnp.float32),
        ],
        in_specs=[smem, smem] + [vmem] * 12,
        out_specs=[vmem] * 4,
        scratch_shapes=[
            pltpu.VMEM((2, tile_r + 2 * half + SUBLANES, tile_c + 2 * half), jnp.float32),
            pltpu.VMEM((slots, 2, width, width), jnp.float32),
            pltpu.VMEM((2, slots * width, width), jnp.bfloat16),
            pltpu.VMEM((2, slots * width, width), jnp.bfloat16),
            pltpu.VMEM((2, width, slots * width), jnp.bfloat16),
            pltpu.VMEM((2, width, slots * width), jnp.bfloat16),
        ],
        compiler_params=pltpu.CompilerParams(vmem_limit_bytes=VMEM_LIMIT),
        cost_estimate=pl.CostEstimate(
            flops=3200000000, bytes_accessed=8000000, transcendentals=131072
        ),
    )(offsets, counts, probe, *map(in_vmem, staged), *map(in_vmem, blocks))


def finish_kernel(*refs):
    (
        specimen, light, low, high, close_low, close_high, far_low, far_high, pair, other,
        fresh, got, specimen_next, probe_next,
    ) = refs
    half = pair.shape[2]
    row_place = lax.axis_index("row")
    col_place = lax.axis_index("col")
    row_odd = lax.rem(row_place, 2)
    col_odd = lax.rem(col_place, 2)
    far_at = row_place + 2 * row_odd - 1
    inside = (far_at >= 0) & (far_at < lax.axis_size("row"))
    for part in range(2):
        sides = (
            (low, close_low, far_low, jnp.where(col_odd == 0, other[part], pair[part])),
            (high, close_high, far_high, jnp.where(col_odd == 0, pair[part], other[part])),
        )
        for side, (own, close, far, rim) in enumerate(sides):
            at = slice(side * half, (side + 1) * half)
            total = own[part] + close[part] + jnp.where(inside, far[part], 0.0) + rim
            specimen_next[part, :, at] = specimen[part, :, at] + total / light[:, at]
        mine, theirs = fresh[part], got[part]
        probe_next[part, :, :LANES] = jnp.where(row_odd == 0, mine, theirs)
        probe_next[part, :, LANES:] = jnp.where(row_odd == 0, theirs, mine)


def finish(specimen, probe, *values):
    vmem = pl.BlockSpec(memory_space=pltpu.VMEM)
    return pl.pallas_call(
        finish_kernel,
        out_shape=[
            jax.ShapeDtypeStruct(specimen.shape, jnp.float32),
            jax.ShapeDtypeStruct(probe.shape, jnp.float32),
        ],
        in_specs=[vmem] * (1 + len(values)),
        out_specs=[vmem] * 2,
        compiler_params=pltpu.CompilerParams(vmem_limit_bytes=VMEM_LIMIT),
        cost_estimate=pl.CostEstimate(flops=1000000, bytes_accessed=3000000, transcendentals=0),
    )(*map(in_vmem, (specimen, *values)))


def in_hbm(value):
    return pltpu.with_memory_space_constraint(value, pltpu.HBM)


def in_vmem(value):
    return pltpu.with_memory_space_constraint(value, pltpu.VMEM)


def fold_kernel(axis, bit, kept_in, got, kept, given):
    layers = 3
    size = (kept.shape[0] - SUBLANES) // layers
    odd = lax.rem(lax.axis_index(axis) // bit, 2)
    for layer in range(layers):
        first = 2 * layer * size
        mine = pl.ds(pl.multiple_of(first + odd * size, SUBLANES), size)
        other = pl.ds(pl.multiple_of(first + (1 - odd) * size, SUBLANES), size)
        at = slice(layer * size, (layer + 1) * size)
        kept[at] = kept_in[mine] + got[mine]
        given[at] = kept_in[other] + got[other]
    total = kept_in[2 * layers * size :] + got[2 * layers * size :]
    kept[layers * size :] = total
    given[layers * size :] = total


def fold(kept, got, axis, bit):
    vmem = pl.BlockSpec(memory_space=pltpu.VMEM)
    shape = jax.ShapeDtypeStruct(((kept.shape[0] + SUBLANES) // 2, LANES), jnp.float32)
    return pl.pallas_call(
        functools.partial(fold_kernel, axis, bit),
        out_shape=[shape] * 2,
        in_specs=[vmem] * 2,
        out_specs=[vmem] * 2,
        compiler_params=pltpu.CompilerParams(vmem_limit_bytes=VMEM_LIMIT),
        cost_estimate=pl.CostEstimate(flops=100000, bytes_accessed=400000, transcendentals=0),
    )(in_vmem(kept), in_vmem(got))


def place(offsets, probe, delta, tile_r, tile_c):
    width = probe.shape[1]
    half = width // 2
    smem = pl.BlockSpec(memory_space=pltpu.SMEM)
    vmem = pl.BlockSpec(memory_space=pltpu.VMEM)
    middle = jax.ShapeDtypeStruct((2, tile_r, tile_c // 2), jnp.float32)
    rim = jax.ShapeDtypeStruct((2, tile_r, half), jnp.float32)
    return pl.pallas_call(
        place_kernel,
        out_shape=[middle, middle, rim, rim] * 3,
        in_specs=[smem, vmem, vmem],
        out_specs=[vmem] * 12,
        scratch_shapes=[
            pltpu.VMEM((2, tile_r + 2 * half + SUBLANES, tile_c + 2 * half), jnp.float32),
        ],
        compiler_params=pltpu.CompilerParams(vmem_limit_bytes=VMEM_LIMIT),
        cost_estimate=pl.CostEstimate(flops=4000000, bytes_accessed=4000000, transcendentals=0),
    )(offsets, probe, delta)


def exchange(value, axis, count, bit):
    return lax.ppermute(value, axis, [(i, i ^ bit) for i in range(count)])


def shards(specimen, probe_field, scan_offsets, live_counts, magnitudes):
    rows, cols = lax.axis_size("row"), lax.axis_size("col")
    width = probe_field.shape[1]
    half = width // 2
    tile_r, tile_c = specimen.shape[1:]
    row_place = lax.axis_index("row")
    col_place = lax.axis_index("col")
    row_odd = row_place % 2
    col_odd = col_place % 2
    pairs = [(i, i ^ 1) for i in range(cols)]
    others = [(i, i + 1) for i in range(1, cols - 1, 2)] + [(i + 1, i) for i in range(1, cols - 1, 2)]
    toward = [(i, i + 2) for i in range(1, rows - 2, 2)] + [(i, i - 2) for i in range(2, rows, 2)]
    toward += [(rows - 1, rows - 2), (0, 1)]
    onward_pairs = [(target, source) for source, target in toward]

    tie = lax.optimization_barrier

    def core(values):
        return [exchange(value, "row", rows, 1) for value in values]

    low, high = specimen[:, :, :half], specimen[:, :, tile_c - half :]
    pair_rim = lax.ppermute(jnp.where(col_odd == 0, high, low), "col", pairs)
    other_rim = lax.ppermute(jnp.where(col_odd == 0, low, high), "col", others)
    late, pair_rim = tie((magnitudes[0, 0], pair_rim))
    staged = stage(late)
    beyond = [lax.ppermute(block, "row", toward) for block in (specimen, pair_rim)]
    other_rim, staged, beyond = tie((other_rim, staged, beyond))
    own = [specimen, pair_rim, other_rim]
    beyond += [lax.ppermute(other_rim, "row", toward)]
    probe_late, other_rim = tie((probe_field, other_rim))
    light = lighting(scan_offsets, live_counts, probe_late, tile_r, tile_c)
    beyond[2], light = tie((beyond[2], light))
    kept, given, own_probe, delta = exit_update(
        scan_offsets, live_counts, probe_field, staged, own + core(own) + core(beyond)
    )

    def pick(condition, first, second):
        return jnp.where(condition, first, second)

    def join(value, axis, count, bit):
        place_here = (lax.axis_index(axis) // bit) % 2
        got = exchange(value, axis, count, bit)
        return pick(
            place_here == 0,
            jnp.concatenate([value, got], 1),
            jnp.concatenate([got, value], 1),
        )

    kept, given = fold(kept, exchange(given, "row", rows, 1), "row", 2)
    given, delta = tie((given, delta))
    parts = place(scan_offsets, probe_field, delta, tile_r, tile_c)
    center, close, onward = parts[:4], parts[4:8], parts[8:]
    got_close, got_onward = core(close), core(onward)
    got = exchange(given, "row", rows, 2)
    kept, given = fold(kept, got, "col", 1)
    given, got_close, got_onward = tie((given, got_close, got_onward))
    beyond = [lax.ppermute(block, "row", onward_pairs) for block in got_onward]
    inside = (row_place + 2 * row_odd - 1 >= 0) & (row_place + 2 * row_odd - 1 < rows)
    value = kept + exchange(given, "col", cols, 1)
    value, *beyond[2:] = tie((value, *beyond[2:]))
    pair_part, other_part = (
        first + second + pick(inside, third, 0.0)
        for first, second, third in zip(center[2:], got_close[2:], beyond[2:])
    )
    other_part = lax.ppermute(other_part, "col", others)
    filled = jnp.concatenate([value, jnp.zeros((64, LANES), jnp.float32)])
    value = value + exchange(filled, "col", cols, 2)[: value.shape[0]]
    value, beyond = tie((value, beyond))
    for bit in (1 << k for k in range(2, cols.bit_length() - 1)):
        value = value + exchange(value, "col", cols, 2 * bit - 2)
    for bit in (1 << k for k in range(2, rows.bit_length() - 1)):
        value = value + exchange(value, "row", rows, bit)
    value, other_part, pair_part = tie((value, other_part, pair_part))
    size = own_probe.shape[1]
    real, imag, weight, total = (value[k * size : (k + 1) * size] for k in range(4))
    update = jnp.stack([real, imag]) / (weight + probe_damping * (total[:1] / (width * width)))
    fresh = own_probe + update
    fresh = join(fresh, "col", cols, 1)
    fresh, pair_part = tie((fresh, pair_part))
    pair_part = lax.ppermute(pair_part, "col", pairs)
    fresh = join(fresh, "row", rows, 2)
    fresh, pair_part = tie((fresh, pair_part))
    got = exchange(fresh, "row", rows, 1)
    return finish(
        specimen, probe_field, light, *center[:2], *got_close[:2], *beyond[:2],
        pair_part, other_part, fresh, got,
    )


def solution(mesh):
    return jax.shard_map(
        shards,
        mesh=mesh,
        in_specs=(P(None, "row", "col"), P(), P(), P(), P("row", "col", None, None, None)),
        out_specs=(P(None, "row", "col"), P()),
        check_vma=False,
    )
```

```python
import functools
import math

import jax
import jax.numpy as jnp
import ml_dtypes
import numpy as np
from jax import lax
from jax.experimental import pallas as pl
from jax.experimental.pallas import tpu as pltpu
from jax.sharding import PartitionSpec as P

modulus_floor = 0.25
object_damping = 0.1
probe_damping = 0.1
LANES = 128
SUBLANES = 8
VMEM_LIMIT = 20 * 1024 * 1024


def dft_tables(width):
    half = width // 2
    counter = np.arange(half)
    tables = []
    for odd in range(2):
        phase = counter[:, None] * (2 * counter[None, :] + odd) % width
        angle = phase * (2.0 * math.pi / width)
        real, imag = np.cos(angle) / math.sqrt(width), -np.sin(angle) / math.sqrt(width)
        tables.append(np.block([[real, imag], [-imag, real]]))
    tables = np.stack(tables + [table.T for table in tables])
    high = tables.astype(ml_dtypes.bfloat16)
    low = (tables - high.astype(np.float64)).astype(ml_dtypes.bfloat16)
    return np.stack([high, low], 1)


def halves(value):
    high = value.astype(jnp.bfloat16)
    return high, (value - high.astype(jnp.float32)).astype(jnp.bfloat16)


def product(left, right):
    dot = functools.partial(jnp.dot, preferred_element_type=jnp.float32)
    return dot(left[0], right[0]) + (dot(left[1], right[0]) + dot(left[0], right[1]))


def keep(ref, rows, lanes, value):
    for place, half in enumerate(halves(value)):
        ref[place, rows, lanes] = half


def product_of(left, right):
    return product((left[0], left[1]), (right[0], right[1]))


def split_start(start, step, last):
    aligned = jnp.minimum(start // step, last // step) * step
    return pl.multiple_of(aligned, step), start - aligned


def lane_groups(value):
    return [value[..., at : at + LANES] for at in range(0, value.shape[-1], LANES)]


def cut(value, row_shift, lane_shift):
    rows, lanes = value.shape
    value = value.reshape(rows // SUBLANES, SUBLANES, lanes)
    lane_turn = lax.rem(LANES - lane_shift, LANES)
    row_turn = lax.rem(SUBLANES - row_shift, SUBLANES)
    shape = (rows // SUBLANES, SUBLANES, LANES)
    keep_lane = lax.broadcasted_iota(jnp.int32, shape, 2) < LANES - lane_shift
    keep_row = lax.broadcasted_iota(jnp.int32, shape, 1)[1:] < SUBLANES - row_shift
    turned = [pltpu.roll(group, lane_turn, 2) for group in lane_groups(value)]
    parts = []
    for first, second in zip(turned[:-1], turned[1:]):
        part = pltpu.roll(jnp.where(keep_lane, first, second), row_turn, 1)
        part = jnp.where(keep_row, part[:-1], part[1:])
        parts.append(part.reshape(rows - SUBLANES, LANES))
    return jnp.concatenate(parts, 1)


def spread(value, row_shift, lane_shift):
    rows, lanes = value.shape
    value = value.reshape(rows // SUBLANES, SUBLANES, lanes)
    shape = (rows // SUBLANES + 1, SUBLANES, LANES)
    lane_turn = lax.rem(lane_shift, LANES)
    take_lane = lax.broadcasted_iota(jnp.int32, shape, 2) < lane_shift
    take_row = lax.broadcasted_iota(jnp.int32, shape, 1) < row_shift
    blank_row = jnp.zeros((1, SUBLANES, LANES), value.dtype)
    turned = []
    for group in lane_groups(value):
        group = pltpu.roll(group, row_shift, 1)
        group = jnp.where(
            take_row,
            jnp.concatenate([blank_row, group], 0),
            jnp.concatenate([group, blank_row], 0),
        )
        turned.append(pltpu.roll(group, lane_turn, 2))
    blank = jnp.zeros(shape, value.dtype)
    parts = [
        jnp.where(take_lane, first, second).reshape(rows + SUBLANES, LANES)
        for first, second in zip([blank] + turned, turned + [blank])
    ]
    return jnp.concatenate(parts, 1)


def lighting_kernel(offsets, counts, probe, out, pad):
    rows, cols, slots = offsets.shape[:3]
    tile_r, tile_c = out.shape
    width = probe.shape[1]
    half = width // 2
    row_place = lax.axis_index("row")
    col_place = lax.axis_index("col")
    power = probe[0] * probe[0] + probe[1] * probe[1]
    pad[...] = jnp.zeros_like(pad)
    pad[tile_r : tile_r + width, tile_c : tile_c + width] = power
    out[...] = jnp.full(out.shape, object_damping * jnp.max(power))
    wide = tile_c + LANES
    for row_step in (-1, 0, 1):
        for col_step in (-1, 0, 1):
            row, col = row_place + row_step, col_place + col_step
            inside = (row >= 0) & (row < rows) & (col >= 0) & (col < cols)
            row_at = jnp.clip(row, 0, rows - 1)
            col_at = jnp.clip(col, 0, cols - 1)
            for slot in range(slots):
                top = offsets[row_at, col_at, slot, 0] + row_step * tile_r
                left = offsets[row_at, col_at, slot, 1] + col_step * tile_c

                @pl.when(
                    inside
                    & (slot < counts[row_at, col_at])
                    & (left > -width)
                    & (left < tile_c)
                )
                def _():
                    row, row_shift = split_start(tile_r - top, SUBLANES, tile_r + width)
                    lane, lane_shift = split_start(tile_c - left, LANES, pad.shape[1] - wide)
                    part = pad[pl.ds(row, tile_r + SUBLANES), pl.ds(lane, wide)]
                    out[...] += cut(part, row_shift, lane_shift)


def lighting(offsets, counts, probe, tile_r, tile_c):
    width = probe.shape[1]
    smem = pl.BlockSpec(memory_space=pltpu.SMEM)
    vmem = pl.BlockSpec(memory_space=pltpu.VMEM)
    return pl.pallas_call(
        lighting_kernel,
        out_shape=jax.ShapeDtypeStruct((tile_r, tile_c), jnp.float32),
        in_specs=[smem, smem, vmem],
        out_specs=vmem,
        scratch_shapes=[
            pltpu.VMEM((2 * tile_r + width + SUBLANES, 2 * tile_c + width), jnp.float32)
        ],
        compiler_params=pltpu.CompilerParams(vmem_limit_bytes=VMEM_LIMIT),
        cost_estimate=pl.CostEstimate(flops=40000000, bytes_accessed=8000000, transcendentals=0),
    )(offsets, counts, probe)


def patch_block(offsets, row_place, col_place, slot, half, tile_r, width):
    row, row_shift = split_start(offsets[row_place, col_place, slot, 0] + half, SUBLANES, tile_r)
    lane, lane_shift = split_start(
        offsets[row_place, col_place, slot, 1] + half, LANES, 2 * half - LANES
    )
    return (pl.ds(row, width + SUBLANES), pl.ds(lane, width + LANES)), row_shift, lane_shift


def delta_kernel(
    offsets, counts, probe, magnitudes, tables,
    own, pair_rim, other_rim, near, near_pair, near_other, far, far_pair, far_other,
    kept, given, own_probe, delta, ext, patches, tall_even, tall_odd, wide_even, wide_odd,
):
    slots, width = magnitudes.shape[0], magnitudes.shape[1]
    half = width // 2
    tile_r, tile_c = own.shape[1:]
    row_place = lax.axis_index("row")
    col_place = lax.axis_index("col")
    row_odd = lax.rem(row_place, 2)
    col_odd = lax.rem(col_place, 2)
    near_row = pl.multiple_of((1 - row_odd) * (tile_r + half), half)
    far_row = pl.multiple_of(row_odd * (tile_r + half), half)
    pair_col = pl.multiple_of((1 - col_odd) * (tile_c + half), half)
    other_col = pl.multiple_of(col_odd * (tile_c + half), half)
    far_at = row_place + 2 * row_odd - 1
    inside = (far_at >= 0) & (far_at < lax.axis_size("row"))
    strips = (
        (half, True, own, pair_rim, other_rim),
        (near_row, True, near, near_pair, near_other),
        (far_row, inside, far, far_pair, far_other),
    )
    for part in range(2):
        for row, valid, *blocks in strips:
            at = pl.ds(row, tile_r)
            mid, pair, other = (
                block[part] if valid is True else jnp.where(valid, block[part], 0.0)
                for block in blocks
            )
            ext[part, at, half : half + tile_c] = mid
            ext[part, at, pl.ds(pair_col, half)] = pair
            ext[part, at, pl.ds(other_col, half)] = other
    live_count = counts[row_place, col_place]
    probe_real, probe_imag = probe[0], probe[1]
    right_even, right_odd, left_even, left_odd = (tables.at[k] for k in range(4))
    low, high = slice(0, half), slice(half, width)
    for slot in range(slots):
        block, row_shift, lane_shift = patch_block(
            offsets, row_place, col_place, slot, half, tile_r, width
        )
        for part in range(2):
            patches[slot, part] = cut(ext[part, *block], row_shift, lane_shift)
        patch_real, patch_imag = patches[slot, 0], patches[slot, 1]
        at = slice(slot * width, (slot + 1) * width)
        for part, wave in (
            (low, probe_real * patch_real - probe_imag * patch_imag),
            (high, probe_real * patch_imag + probe_imag * patch_real),
        ):
            keep(tall_even, at, part, wave[:, low] + wave[:, high])
            keep(tall_odd, at, part, wave[:, low] - wave[:, high])
    inner = (product_of(tall_even, right_even), product_of(tall_odd, right_odd))
    for slot in range(slots):
        top = slice(slot * width, slot * width + half)
        bottom = slice(slot * width + half, (slot + 1) * width)
        for odd in range(2):
            at = slice(slot * width + odd * half, slot * width + (odd + 1) * half)
            for part in (low, high):
                upper, lower = inner[odd][top, part], inner[odd][bottom, part]
                keep(wide_even, part, at, upper + lower)
                keep(wide_odd, part, at, upper - lower)
    outer = (product_of(left_even, wide_even), product_of(left_odd, wide_odd))
    for slot in range(slots):
        lanes = slice(slot * width, (slot + 1) * width)
        for odd in range(2):
            far_real, far_imag = outer[odd][low, lanes], outer[odd][high, lanes]
            inverse = jnp.minimum(
                lax.rsqrt(far_real * far_real + far_imag * far_imag), 1.0 / modulus_floor
            )
            factor = magnitudes[slot, odd * half : (odd + 1) * half] * inverse - 1.0
            at = slice(slot * width + odd * half, slot * width + (odd + 1) * half)
            for part, back in ((low, far_real * factor), (high, far_imag * factor)):
                keep(tall_even, at, part, back[:, low])
                keep(tall_odd, at, part, back[:, high])
    inner = (product_of(tall_even, left_even), product_of(tall_odd, left_odd))
    for slot in range(slots):
        for odd, ref in enumerate((wide_even, wide_odd)):
            at = slice(slot * width + odd * half, slot * width + (odd + 1) * half)
            for part in (low, high):
                one, other = inner[0][at, part], inner[1][at, part]
                keep(ref, part, slice(slot * width, slot * width + half), one + other)
                keep(ref, part, slice(slot * width + half, (slot + 1) * width), one - other)
    outer = (product_of(right_even, wide_even), product_of(right_odd, wide_odd))
    sums = [jnp.zeros((width, width), jnp.float32)] * 3
    for slot in range(slots):
        live = jnp.where(slot < live_count, 1.0, 0.0)
        lanes = slice(slot * width, (slot + 1) * width)
        for part, rows in enumerate((low, high)):
            one, other = outer[0][rows, lanes], outer[1][rows, lanes]
            delta[slot, part, low] = (one + other) * live
            delta[slot, part, high] = (one - other) * live
        delta_real, delta_imag = delta[slot, 0], delta[slot, 1]
        patch_real, patch_imag = patches[slot, 0], patches[slot, 1]
        sums = [
            sums[0] + (patch_real * delta_real + patch_imag * delta_imag),
            sums[1] + (patch_real * delta_imag - patch_imag * delta_real),
            sums[2] + live * (patch_real * patch_real + patch_imag * patch_imag),
        ]
    even = row_odd == 0
    for layer in range(3):
        one, other = lane_groups(sums[layer])
        kept[layer * width : (layer + 1) * width] = jnp.where(even, one, other)
        given[layer * width : (layer + 1) * width] = jnp.where(even, other, one)
    total = jnp.full((SUBLANES, LANES), jnp.sum(sums[2]))
    kept[3 * width :] = total
    given[3 * width :] = total
    size = own_probe.shape[1]
    row = pl.multiple_of(lax.rem(row_place // 2, 2) * (2 * size) + col_odd * size, size)
    for part in range(2):
        one, other = lane_groups(probe[part, pl.ds(row, size), :])
        own_probe[part] = jnp.where(even, one, other)


def place_kernel(
    offsets, probe, delta, *blocks_and_ext
):
    *blocks, ext = blocks_and_ext
    slots, width = delta.shape[0], delta.shape[2]
    half = width // 2
    tile_r = blocks[0].shape[1]
    tile_c = ext.shape[2] - 2 * half
    row_place = lax.axis_index("row")
    col_place = lax.axis_index("col")
    row_odd = lax.rem(row_place, 2)
    col_odd = lax.rem(col_place, 2)
    ext[...] = jnp.zeros_like(ext)
    probe_real, probe_imag = probe[0], probe[1]
    for slot in range(slots):
        real, imag = delta[slot, 0], delta[slot, 1]
        block, row_shift, lane_shift = patch_block(
            offsets, row_place, col_place, slot, half, tile_r, width
        )
        for part, grad in enumerate(
            (probe_real * real + probe_imag * imag, probe_real * imag - probe_imag * real)
        ):
            ext[part, *block] += spread(grad, row_shift, lane_shift)
    near_row = pl.multiple_of((1 - row_odd) * (tile_r + half), half)
    far_row = pl.multiple_of(row_odd * (tile_r + half), half)
    pair_col = pl.multiple_of((1 - col_odd) * (tile_c + half), half)
    other_col = pl.multiple_of(col_odd * (tile_c + half), half)
    for k, row in enumerate((half, near_row, far_row)):
        low, high, pair, other = blocks[4 * k : 4 * k + 4]
        at = pl.ds(row, tile_r)
        low[...] = ext[:, at, half : half + tile_c // 2]
        high[...] = ext[:, at, half + tile_c // 2 : half + tile_c]
        pair[...] = ext[:, at, pl.ds(pair_col, half)]
        other[...] = ext[:, at, pl.ds(other_col, half)]


def stage_kernel(magnitudes, tables, ordered, held, measured, arrived):
    slots, width = magnitudes.shape[:2]
    copies = [
        pltpu.make_async_copy(tables, held, arrived.at[0]),
        pltpu.make_async_copy(magnitudes, measured, arrived.at[1]),
    ]
    for copy in copies:
        copy.start()
    line = lax.broadcasted_iota(jnp.int32, (width, width), 0)
    place = lax.broadcasted_iota(jnp.int32, (width, width), 1)

    def chosen(here, there):
        source = jnp.where(here < width // 2, 2 * here, 2 * here - (width - 1))
        return jnp.where(source == there, 1.0, 0.0).astype(jnp.bfloat16)

    by_row, by_lane = chosen(line, place), chosen(place, line)
    copies[1].wait()
    for slot in range(slots):
        rest = measured[slot]
        total = jnp.zeros((width, width), jnp.float32)
        for _ in range(3):
            piece = rest.astype(jnp.bfloat16)
            rest = rest - piece.astype(jnp.float32)
            piece = jnp.dot(by_row, piece, preferred_element_type=jnp.float32)
            total += jnp.dot(
                piece.astype(jnp.bfloat16), by_lane, preferred_element_type=jnp.float32
            )
        ordered[slot] = total
    copies[0].wait()


def stage(magnitudes):
    width = magnitudes.shape[-1]
    hbm = pl.BlockSpec(memory_space=pltpu.HBM)
    vmem = pl.BlockSpec(memory_space=pltpu.VMEM)
    return pl.pallas_call(
        stage_kernel,
        out_shape=[
            jax.ShapeDtypeStruct(magnitudes.shape, jnp.float32),
            jax.ShapeDtypeStruct((4, 2, width, width), jnp.bfloat16),
        ],
        in_specs=[hbm] * 2,
        out_specs=[vmem] * 2,
        scratch_shapes=[
            pltpu.VMEM(magnitudes.shape, jnp.float32),
            pltpu.SemaphoreType.DMA((2,)),
        ],
        compiler_params=pltpu.CompilerParams(vmem_limit_bytes=VMEM_LIMIT),
        cost_estimate=pl.CostEstimate(flops=400000000, bytes_accessed=3000000, transcendentals=0),
    )(in_hbm(magnitudes), in_hbm(jnp.asarray(dft_tables(width))))


def exit_update(offsets, counts, probe, staged, blocks):
    slots, width = staged[0].shape[:2]
    own = blocks[0]
    half = width // 2
    tile_r, tile_c = own.shape[1:]
    smem = pl.BlockSpec(memory_space=pltpu.SMEM)
    vmem = pl.BlockSpec(memory_space=pltpu.VMEM)
    return pl.pallas_call(
        delta_kernel,
        out_shape=[
            jax.ShapeDtypeStruct((3 * width + SUBLANES, LANES), jnp.float32),
            jax.ShapeDtypeStruct((3 * width + SUBLANES, LANES), jnp.float32),
            jax.ShapeDtypeStruct((2, width // 4, LANES), jnp.float32),
            jax.ShapeDtypeStruct((slots, 2, width, width), jnp.float32),
        ],
        in_specs=[smem, smem] + [vmem] * 12,
        out_specs=[vmem] * 4,
        scratch_shapes=[
            pltpu.VMEM((2, tile_r + 2 * half + SUBLANES, tile_c + 2 * half), jnp.float32),
            pltpu.VMEM((slots, 2, width, width), jnp.float32),
            pltpu.VMEM((2, slots * width, width), jnp.bfloat16),
            pltpu.VMEM((2, slots * width, width), jnp.bfloat16),
            pltpu.VMEM((2, width, slots * width), jnp.bfloat16),
            pltpu.VMEM((2, width, slots * width), jnp.bfloat16),
        ],
        compiler_params=pltpu.CompilerParams(vmem_limit_bytes=VMEM_LIMIT),
        cost_estimate=pl.CostEstimate(
            flops=3200000000, bytes_accessed=8000000, transcendentals=131072
        ),
    )(offsets, counts, probe, *map(in_vmem, staged), *map(in_vmem, blocks))


def finish_kernel(*refs):
    (
        specimen, light, low, high, close_low, close_high, far_low, far_high, pair, other,
        fresh, got, specimen_next, probe_next,
    ) = refs
    half = pair.shape[2]
    row_place = lax.axis_index("row")
    col_place = lax.axis_index("col")
    row_odd = lax.rem(row_place, 2)
    col_odd = lax.rem(col_place, 2)
    far_at = row_place + 2 * row_odd - 1
    inside = (far_at >= 0) & (far_at < lax.axis_size("row"))
    for part in range(2):
        sides = (
            (low, close_low, far_low, jnp.where(col_odd == 0, other[part], pair[part])),
            (high, close_high, far_high, jnp.where(col_odd == 0, pair[part], other[part])),
        )
        for side, (own, close, far, rim) in enumerate(sides):
            at = slice(side * half, (side + 1) * half)
            total = own[part] + close[part] + jnp.where(inside, far[part], 0.0) + rim
            specimen_next[part, :, at] = specimen[part, :, at] + total / light[:, at]
        mine, theirs = fresh[part], got[part]
        probe_next[part, :, :LANES] = jnp.where(row_odd == 0, mine, theirs)
        probe_next[part, :, LANES:] = jnp.where(row_odd == 0, theirs, mine)


def finish(specimen, probe, *values):
    vmem = pl.BlockSpec(memory_space=pltpu.VMEM)
    return pl.pallas_call(
        finish_kernel,
        out_shape=[
            jax.ShapeDtypeStruct(specimen.shape, jnp.float32),
            jax.ShapeDtypeStruct(probe.shape, jnp.float32),
        ],
        in_specs=[vmem] * (1 + len(values)),
        out_specs=[vmem] * 2,
        compiler_params=pltpu.CompilerParams(vmem_limit_bytes=VMEM_LIMIT),
        cost_estimate=pl.CostEstimate(flops=1000000, bytes_accessed=3000000, transcendentals=0),
    )(*map(in_vmem, (specimen, *values)))


def in_hbm(value):
    return pltpu.with_memory_space_constraint(value, pltpu.HBM)


def in_vmem(value):
    return pltpu.with_memory_space_constraint(value, pltpu.VMEM)


def fold_kernel(axis, bit, kept_in, got, kept, given):
    layers = 3
    size = (kept.shape[0] - SUBLANES) // layers
    odd = lax.rem(lax.axis_index(axis) // bit, 2)
    for layer in range(layers):
        first = 2 * layer * size
        mine = pl.ds(pl.multiple_of(first + odd * size, SUBLANES), size)
        other = pl.ds(pl.multiple_of(first + (1 - odd) * size, SUBLANES), size)
        at = slice(layer * size, (layer + 1) * size)
        kept[at] = kept_in[mine] + got[mine]
        given[at] = kept_in[other] + got[other]
    total = kept_in[2 * layers * size :] + got[2 * layers * size :]
    kept[layers * size :] = total
    given[layers * size :] = total


def fold(kept, got, axis, bit):
    vmem = pl.BlockSpec(memory_space=pltpu.VMEM)
    shape = jax.ShapeDtypeStruct(((kept.shape[0] + SUBLANES) // 2, LANES), jnp.float32)
    return pl.pallas_call(
        functools.partial(fold_kernel, axis, bit),
        out_shape=[shape] * 2,
        in_specs=[vmem] * 2,
        out_specs=[vmem] * 2,
        compiler_params=pltpu.CompilerParams(vmem_limit_bytes=VMEM_LIMIT),
        cost_estimate=pl.CostEstimate(flops=100000, bytes_accessed=400000, transcendentals=0),
    )(in_vmem(kept), in_vmem(got))


def place(offsets, probe, delta, tile_r, tile_c):
    width = probe.shape[1]
    half = width // 2
    smem = pl.BlockSpec(memory_space=pltpu.SMEM)
    vmem = pl.BlockSpec(memory_space=pltpu.VMEM)
    middle = jax.ShapeDtypeStruct((2, tile_r, tile_c // 2), jnp.float32)
    rim = jax.ShapeDtypeStruct((2, tile_r, half), jnp.float32)
    return pl.pallas_call(
        place_kernel,
        out_shape=[middle, middle, rim, rim] * 3,
        in_specs=[smem, vmem, vmem],
        out_specs=[vmem] * 12,
        scratch_shapes=[
            pltpu.VMEM((2, tile_r + 2 * half + SUBLANES, tile_c + 2 * half), jnp.float32),
        ],
        compiler_params=pltpu.CompilerParams(vmem_limit_bytes=VMEM_LIMIT),
        cost_estimate=pl.CostEstimate(flops=4000000, bytes_accessed=4000000, transcendentals=0),
    )(offsets, probe, delta)


def exchange(value, axis, count, bit):
    return lax.ppermute(value, axis, [(i, i ^ bit) for i in range(count)])


def shards(specimen, probe_field, scan_offsets, live_counts, magnitudes):
    rows, cols = lax.axis_size("row"), lax.axis_size("col")
    width = probe_field.shape[1]
    half = width // 2
    tile_r, tile_c = specimen.shape[1:]
    row_place = lax.axis_index("row")
    col_place = lax.axis_index("col")
    row_odd = row_place % 2
    col_odd = col_place % 2
    pairs = [(i, i ^ 1) for i in range(cols)]
    others = [(i, i + 1) for i in range(1, cols - 1, 2)] + [(i + 1, i) for i in range(1, cols - 1, 2)]
    toward = [(i, i + 2) for i in range(1, rows - 2, 2)] + [(i, i - 2) for i in range(2, rows, 2)]
    toward += [(rows - 1, rows - 2), (0, 1)]
    onward_pairs = [(target, source) for source, target in toward]

    tie = lax.optimization_barrier

    def core(values):
        return [exchange(value, "row", rows, 1) for value in values]

    low, high = specimen[:, :, :half], specimen[:, :, tile_c - half :]
    pair_rim = lax.ppermute(jnp.where(col_odd == 0, high, low), "col", pairs)
    other_rim = lax.ppermute(jnp.where(col_odd == 0, low, high), "col", others)
    late, pair_rim = tie((magnitudes[0, 0], pair_rim))
    staged = stage(late)
    beyond = [lax.ppermute(block, "row", toward) for block in (specimen, pair_rim)]
    other_rim, staged, beyond = tie((other_rim, staged, beyond))
    own = [specimen, pair_rim, other_rim]
    beyond += [lax.ppermute(other_rim, "row", toward)]
    probe_late, other_rim = tie((probe_field, other_rim))
    light = lighting(scan_offsets, live_counts, probe_late, tile_r, tile_c)
    beyond[2], light = tie((beyond[2], light))
    kept, given, own_probe, delta = exit_update(
        scan_offsets, live_counts, probe_field, staged, own + core(own) + core(beyond)
    )

    def pick(condition, first, second):
        return jnp.where(condition, first, second)

    square = [
        (r * cols + c, (r ^ 2) * cols + (c ^ 1)) for r in range(rows) for c in range(cols)
    ]

    def all_three(across, beside, diagonal):
        diagonal = lax.ppermute(diagonal, ("row", "col"), square)
        return exchange(across, "row", rows, 2), exchange(beside, "col", cols, 1), diagonal

    kept, given = fold(kept, exchange(given, "row", rows, 1), "row", 2)
    given, delta = tie((given, delta))
    parts = place(scan_offsets, probe_field, delta, tile_r, tile_c)
    center, close, onward = parts[:4], parts[4:8], parts[8:]
    got_close, got_onward = core(close), core(onward)
    got = exchange(given, "row", rows, 2)
    kept, given = fold(kept, got, "col", 1)
    given, got_close, got_onward = tie((given, got_close, got_onward))
    beyond = [lax.ppermute(block, "row", onward_pairs) for block in got_onward]
    inside = (row_place + 2 * row_odd - 1 >= 0) & (row_place + 2 * row_odd - 1 < rows)
    value = kept + exchange(given, "col", cols, 1)
    value, *beyond[2:] = tie((value, *beyond[2:]))
    pair_part, other_part = (
        first + second + pick(inside, third, 0.0)
        for first, second, third in zip(center[2:], got_close[2:], beyond[2:])
    )
    other_part = lax.ppermute(other_part, "col", others)
    filled = jnp.concatenate([value, jnp.zeros((64, LANES), jnp.float32)])
    value = value + exchange(filled, "col", cols, 2)[: value.shape[0]]
    value, beyond = tie((value, beyond))
    for bit in (1 << k for k in range(2, cols.bit_length() - 1)):
        value = value + exchange(value, "col", cols, 2 * bit - 2)
    for bit in (1 << k for k in range(2, rows.bit_length() - 1)):
        value = value + exchange(value, "row", rows, bit)
    value, other_part, pair_part = tie((value, other_part, pair_part))
    size = own_probe.shape[1]
    real, imag, weight, total = (value[k * size : (k + 1) * size] for k in range(4))
    update = jnp.stack([real, imag]) / (weight + probe_damping * (total[:1] / (width * width)))
    fresh = own_probe + update
    pair_part = lax.ppermute(pair_part, "col", pairs)
    across, beside, diagonal = all_three(fresh, fresh, fresh)

    def ordered(place_here, one, other):
        return pick(
            place_here == 0,
            jnp.concatenate([one, other], 1),
            jnp.concatenate([other, one], 1),
        )

    fresh = ordered(
        (row_place // 2) % 2, ordered(col_odd, fresh, beside), ordered(col_odd, across, diagonal)
    )
    fresh, pair_part = tie((fresh, pair_part))
    got = exchange(fresh, "row", rows, 1)
    return finish(
        specimen, probe_field, light, *center[:2], *got_close[:2], *beyond[:2],
        pair_part, other_part, fresh, got,
    )


def solution(mesh):
    return jax.shard_map(
        shards,
        mesh=mesh,
        in_specs=(P(None, "row", "col"), P(), P(), P(), P("row", "col", None, None, None)),
        out_specs=(P(None, "row", "col"), P()),
        check_vma=False,
    )
```

```python
import functools
import math

import jax
import jax.numpy as jnp
import ml_dtypes
import numpy as np
from jax import lax
from jax.experimental import pallas as pl
from jax.experimental.pallas import tpu as pltpu
from jax.sharding import PartitionSpec as P

modulus_floor = 0.25
object_damping = 0.1
probe_damping = 0.1
LANES = 128
SUBLANES = 8
VMEM_LIMIT = 20 * 1024 * 1024


def dft_tables(width):
    half = width // 2
    counter = np.arange(half)
    tables = []
    for odd in range(2):
        phase = counter[:, None] * (2 * counter[None, :] + odd) % width
        angle = phase * (2.0 * math.pi / width)
        real, imag = np.cos(angle) / math.sqrt(width), -np.sin(angle) / math.sqrt(width)
        tables.append(np.block([[real, imag], [-imag, real]]))
    tables = np.stack(tables + [table.T for table in tables])
    high = tables.astype(ml_dtypes.bfloat16)
    low = (tables - high.astype(np.float64)).astype(ml_dtypes.bfloat16)
    return np.stack([high, low], 1)


def halves(value):
    high = value.astype(jnp.bfloat16)
    return high, (value - high.astype(jnp.float32)).astype(jnp.bfloat16)


def product(left, right):
    dot = functools.partial(jnp.dot, preferred_element_type=jnp.float32)
    return dot(left[0], right[0]) + (dot(left[1], right[0]) + dot(left[0], right[1]))


def keep(ref, rows, lanes, value):
    for place, half in enumerate(halves(value)):
        ref[place, rows, lanes] = half


def product_of(left, right):
    return product((left[0], left[1]), (right[0], right[1]))


def split_start(start, step, last):
    aligned = jnp.minimum(start // step, last // step) * step
    return pl.multiple_of(aligned, step), start - aligned


def lane_groups(value):
    return [value[..., at : at + LANES] for at in range(0, value.shape[-1], LANES)]


def cut(value, row_shift, lane_shift):
    rows, lanes = value.shape
    value = value.reshape(rows // SUBLANES, SUBLANES, lanes)
    lane_turn = lax.rem(LANES - lane_shift, LANES)
    row_turn = lax.rem(SUBLANES - row_shift, SUBLANES)
    shape = (rows // SUBLANES, SUBLANES, LANES)
    keep_lane = lax.broadcasted_iota(jnp.int32, shape, 2) < LANES - lane_shift
    keep_row = lax.broadcasted_iota(jnp.int32, shape, 1)[1:] < SUBLANES - row_shift
    turned = [pltpu.roll(group, lane_turn, 2) for group in lane_groups(value)]
    parts = []
    for first, second in zip(turned[:-1], turned[1:]):
        part = pltpu.roll(jnp.where(keep_lane, first, second), row_turn, 1)
        part = jnp.where(keep_row, part[:-1], part[1:])
        parts.append(part.reshape(rows - SUBLANES, LANES))
    return jnp.concatenate(parts, 1)


def spread(value, row_shift, lane_shift):
    rows, lanes = value.shape
    value = value.reshape(rows // SUBLANES, SUBLANES, lanes)
    shape = (rows // SUBLANES + 1, SUBLANES, LANES)
    lane_turn = lax.rem(lane_shift, LANES)
    take_lane = lax.broadcasted_iota(jnp.int32, shape, 2) < lane_shift
    take_row = lax.broadcasted_iota(jnp.int32, shape, 1) < row_shift
    blank_row = jnp.zeros((1, SUBLANES, LANES), value.dtype)
    turned = []
    for group in lane_groups(value):
        group = pltpu.roll(group, row_shift, 1)
        group = jnp.where(
            take_row,
            jnp.concatenate([blank_row, group], 0),
            jnp.concatenate([group, blank_row], 0),
        )
        turned.append(pltpu.roll(group, lane_turn, 2))
    blank = jnp.zeros(shape, value.dtype)
    parts = [
        jnp.where(take_lane, first, second).reshape(rows + SUBLANES, LANES)
        for first, second in zip([blank] + turned, turned + [blank])
    ]
    return jnp.concatenate(parts, 1)


def lighting_kernel(offsets, counts, probe, out, pad):
    rows, cols, slots = offsets.shape[:3]
    tile_r, tile_c = out.shape
    width = probe.shape[1]
    half = width // 2
    row_place = lax.axis_index("row")
    col_place = lax.axis_index("col")
    power = probe[0] * probe[0] + probe[1] * probe[1]
    pad[...] = jnp.zeros_like(pad)
    pad[tile_r : tile_r + width, tile_c : tile_c + width] = power
    out[...] = jnp.full(out.shape, object_damping * jnp.max(power))
    wide = tile_c + LANES
    for row_step in (-1, 0, 1):
        for col_step in (-1, 0, 1):
            row, col = row_place + row_step, col_place + col_step
            inside = (row >= 0) & (row < rows) & (col >= 0) & (col < cols)
            row_at = jnp.clip(row, 0, rows - 1)
            col_at = jnp.clip(col, 0, cols - 1)
            for slot in range(slots):
                top = offsets[row_at, col_at, slot, 0] + row_step * tile_r
                left = offsets[row_at, col_at, slot, 1] + col_step * tile_c

                @pl.when(
                    inside
                    & (slot < counts[row_at, col_at])
                    & (left > -width)
                    & (left < tile_c)
                )
                def _():
                    row, row_shift = split_start(tile_r - top, SUBLANES, tile_r + width)
                    lane, lane_shift = split_start(tile_c - left, LANES, pad.shape[1] - wide)
                    part = pad[pl.ds(row, tile_r + SUBLANES), pl.ds(lane, wide)]
                    out[...] += cut(part, row_shift, lane_shift)


def lighting(offsets, counts, probe, tile_r, tile_c):
    width = probe.shape[1]
    smem = pl.BlockSpec(memory_space=pltpu.SMEM)
    vmem = pl.BlockSpec(memory_space=pltpu.VMEM)
    return pl.pallas_call(
        lighting_kernel,
        out_shape=jax.ShapeDtypeStruct((tile_r, tile_c), jnp.float32),
        in_specs=[smem, smem, vmem],
        out_specs=vmem,
        scratch_shapes=[
            pltpu.VMEM((2 * tile_r + width + SUBLANES, 2 * tile_c + width), jnp.float32)
        ],
        compiler_params=pltpu.CompilerParams(vmem_limit_bytes=VMEM_LIMIT),
        cost_estimate=pl.CostEstimate(flops=40000000, bytes_accessed=8000000, transcendentals=0),
    )(offsets, counts, probe)


def patch_block(offsets, row_place, col_place, slot, half, tile_r, width):
    row, row_shift = split_start(offsets[row_place, col_place, slot, 0] + half, SUBLANES, tile_r)
    lane, lane_shift = split_start(
        offsets[row_place, col_place, slot, 1] + half, LANES, 2 * half - LANES
    )
    return (pl.ds(row, width + SUBLANES), pl.ds(lane, width + LANES)), row_shift, lane_shift


def delta_kernel(
    offsets, counts, probe, magnitudes, tables,
    own, pair_rim, other_rim, near, near_pair, near_other, far, far_pair, far_other,
    kept, given, own_probe, delta, ext, patches, tall_even, tall_odd, wide_even, wide_odd,
):
    slots, width = magnitudes.shape[0], magnitudes.shape[1]
    half = width // 2
    tile_r, tile_c = own.shape[1:]
    row_place = lax.axis_index("row")
    col_place = lax.axis_index("col")
    row_odd = lax.rem(row_place, 2)
    col_odd = lax.rem(col_place, 2)
    near_row = pl.multiple_of((1 - row_odd) * (tile_r + half), half)
    far_row = pl.multiple_of(row_odd * (tile_r + half), half)
    pair_col = pl.multiple_of((1 - col_odd) * (tile_c + half), half)
    other_col = pl.multiple_of(col_odd * (tile_c + half), half)
    far_at = row_place + 2 * row_odd - 1
    inside = (far_at >= 0) & (far_at < lax.axis_size("row"))
    strips = (
        (half, True, own, pair_rim, other_rim),
        (near_row, True, near, near_pair, near_other),
        (far_row, inside, far, far_pair, far_other),
    )
    for part in range(2):
        for row, valid, *blocks in strips:
            at = pl.ds(row, tile_r)
            mid, pair, other = (
                block[part] if valid is True else jnp.where(valid, block[part], 0.0)
                for block in blocks
            )
            ext[part, at, half : half + tile_c] = mid
            ext[part, at, pl.ds(pair_col, half)] = pair
            ext[part, at, pl.ds(other_col, half)] = other
    live_count = counts[row_place, col_place]
    probe_real, probe_imag = probe[0], probe[1]
    right_even, right_odd, left_even, left_odd = (tables.at[k] for k in range(4))
    low, high = slice(0, half), slice(half, width)
    for slot in range(slots):
        block, row_shift, lane_shift = patch_block(
            offsets, row_place, col_place, slot, half, tile_r, width
        )
        for part in range(2):
            patches[slot, part] = cut(ext[part, *block], row_shift, lane_shift)
        patch_real, patch_imag = patches[slot, 0], patches[slot, 1]
        at = slice(slot * width, (slot + 1) * width)
        for part, wave in (
            (low, probe_real * patch_real - probe_imag * patch_imag),
            (high, probe_real * patch_imag + probe_imag * patch_real),
        ):
            keep(tall_even, at, part, wave[:, low] + wave[:, high])
            keep(tall_odd, at, part, wave[:, low] - wave[:, high])
    inner = (product_of(tall_even, right_even), product_of(tall_odd, right_odd))
    for slot in range(slots):
        top = slice(slot * width, slot * width + half)
        bottom = slice(slot * width + half, (slot + 1) * width)
        for odd in range(2):
            at = slice(slot * width + odd * half, slot * width + (odd + 1) * half)
            for part in (low, high):
                upper, lower = inner[odd][top, part], inner[odd][bottom, part]
                keep(wide_even, part, at, upper + lower)
                keep(wide_odd, part, at, upper - lower)
    outer = (product_of(left_even, wide_even), product_of(left_odd, wide_odd))
    for slot in range(slots):
        lanes = slice(slot * width, (slot + 1) * width)
        for odd in range(2):
            far_real, far_imag = outer[odd][low, lanes], outer[odd][high, lanes]
            inverse = jnp.minimum(
                lax.rsqrt(far_real * far_real + far_imag * far_imag), 1.0 / modulus_floor
            )
            factor = magnitudes[slot, odd * half : (odd + 1) * half] * inverse - 1.0
            at = slice(slot * width + odd * half, slot * width + (odd + 1) * half)
            for part, back in ((low, far_real * factor), (high, far_imag * factor)):
                keep(tall_even, at, part, back[:, low])
                keep(tall_odd, at, part, back[:, high])
    inner = (product_of(tall_even, left_even), product_of(tall_odd, left_odd))
    for slot in range(slots):
        for odd, ref in enumerate((wide_even, wide_odd)):
            at = slice(slot * width + odd * half, slot * width + (odd + 1) * half)
            for part in (low, high):
                one, other = inner[0][at, part], inner[1][at, part]
                keep(ref, part, slice(slot * width, slot * width + half), one + other)
                keep(ref, part, slice(slot * width + half, (slot + 1) * width), one - other)
    outer = (product_of(right_even, wide_even), product_of(right_odd, wide_odd))
    sums = [jnp.zeros((width, width), jnp.float32)] * 3
    for slot in range(slots):
        live = jnp.where(slot < live_count, 1.0, 0.0)
        lanes = slice(slot * width, (slot + 1) * width)
        for part, rows in enumerate((low, high)):
            one, other = outer[0][rows, lanes], outer[1][rows, lanes]
            delta[slot, part, low] = (one + other) * live
            delta[slot, part, high] = (one - other) * live
        delta_real, delta_imag = delta[slot, 0], delta[slot, 1]
        patch_real, patch_imag = patches[slot, 0], patches[slot, 1]
        sums = [
            sums[0] + (patch_real * delta_real + patch_imag * delta_imag),
            sums[1] + (patch_real * delta_imag - patch_imag * delta_real),
            sums[2] + live * (patch_real * patch_real + patch_imag * patch_imag),
        ]
    even = row_odd == 0
    for layer in range(3):
        one, other = lane_groups(sums[layer])
        kept[layer * width : (layer + 1) * width] = jnp.where(even, one, other)
        given[layer * width : (layer + 1) * width] = jnp.where(even, other, one)
    total = jnp.full((SUBLANES, LANES), jnp.sum(sums[2]))
    kept[3 * width :] = total
    given[3 * width :] = total
    size = own_probe.shape[1]
    row = pl.multiple_of(lax.rem(row_place // 2, 2) * (2 * size) + col_odd * size, size)
    for part in range(2):
        one, other = lane_groups(probe[part, pl.ds(row, size), :])
        own_probe[part] = jnp.where(even, one, other)


def place_kernel(
    offsets, probe, delta, *blocks_and_ext
):
    center_mid, center_rim, packet, ext = blocks_and_ext
    slots, width = delta.shape[0], delta.shape[2]
    half = width // 2
    tile_r = center_mid.shape[1]
    tile_c = ext.shape[2] - 2 * half
    row_place = lax.axis_index("row")
    col_place = lax.axis_index("col")
    row_odd = lax.rem(row_place, 2)
    col_odd = lax.rem(col_place, 2)
    ext[...] = jnp.zeros_like(ext)
    probe_real, probe_imag = probe[0], probe[1]
    for slot in range(slots):
        real, imag = delta[slot, 0], delta[slot, 1]
        block, row_shift, lane_shift = patch_block(
            offsets, row_place, col_place, slot, half, tile_r, width
        )
        for part, grad in enumerate(
            (probe_real * real + probe_imag * imag, probe_real * imag - probe_imag * real)
        ):
            ext[part, *block] += spread(grad, row_shift, lane_shift)
    near_row = pl.multiple_of((1 - row_odd) * (tile_r + half), half)
    far_row = pl.multiple_of(row_odd * (tile_r + half), half)
    pair_col = pl.multiple_of((1 - col_odd) * (tile_c + half), half)
    other_col = pl.multiple_of(col_odd * (tile_c + half), half)
    middle = tile_c // 2
    for row, rim, mid in (
        (half, center_rim, center_mid),
        (far_row, packet.at[0:4], packet.at[4:8]),
        (near_row, packet.at[8:12], packet.at[12:16]),
    ):
        at = pl.ds(row, tile_r)
        mid[0:2] = ext[:, at, half : half + middle]
        mid[2:4] = ext[:, at, half + middle : half + tile_c]
        rim[0:2] = ext[:, at, pl.ds(pair_col, half)]
        rim[2:4] = ext[:, at, pl.ds(other_col, half)]


def stage_kernel(magnitudes, tables, ordered, held, measured, arrived):
    slots, width = magnitudes.shape[:2]
    copies = [
        pltpu.make_async_copy(tables, held, arrived.at[0]),
        pltpu.make_async_copy(magnitudes, measured, arrived.at[1]),
    ]
    for copy in copies:
        copy.start()
    line = lax.broadcasted_iota(jnp.int32, (width, width), 0)
    place = lax.broadcasted_iota(jnp.int32, (width, width), 1)

    def chosen(here, there):
        source = jnp.where(here < width // 2, 2 * here, 2 * here - (width - 1))
        return jnp.where(source == there, 1.0, 0.0).astype(jnp.bfloat16)

    by_row, by_lane = chosen(line, place), chosen(place, line)
    copies[1].wait()
    for slot in range(slots):
        rest = measured[slot]
        total = jnp.zeros((width, width), jnp.float32)
        for _ in range(3):
            piece = rest.astype(jnp.bfloat16)
            rest = rest - piece.astype(jnp.float32)
            piece = jnp.dot(by_row, piece, preferred_element_type=jnp.float32)
            total += jnp.dot(
                piece.astype(jnp.bfloat16), by_lane, preferred_element_type=jnp.float32
            )
        ordered[slot] = total
    copies[0].wait()


def stage(magnitudes):
    width = magnitudes.shape[-1]
    hbm = pl.BlockSpec(memory_space=pltpu.HBM)
    vmem = pl.BlockSpec(memory_space=pltpu.VMEM)
    return pl.pallas_call(
        stage_kernel,
        out_shape=[
            jax.ShapeDtypeStruct(magnitudes.shape, jnp.float32),
            jax.ShapeDtypeStruct((4, 2, width, width), jnp.bfloat16),
        ],
        in_specs=[hbm] * 2,
        out_specs=[vmem] * 2,
        scratch_shapes=[
            pltpu.VMEM(magnitudes.shape, jnp.float32),
            pltpu.SemaphoreType.DMA((2,)),
        ],
        compiler_params=pltpu.CompilerParams(vmem_limit_bytes=VMEM_LIMIT),
        cost_estimate=pl.CostEstimate(flops=400000000, bytes_accessed=3000000, transcendentals=0),
    )(in_hbm(magnitudes), in_hbm(jnp.asarray(dft_tables(width))))


def exit_update(offsets, counts, probe, staged, blocks):
    slots, width = staged[0].shape[:2]
    own = blocks[0]
    half = width // 2
    tile_r, tile_c = own.shape[1:]
    smem = pl.BlockSpec(memory_space=pltpu.SMEM)
    vmem = pl.BlockSpec(memory_space=pltpu.VMEM)
    return pl.pallas_call(
        delta_kernel,
        out_shape=[
            jax.ShapeDtypeStruct((3 * width + SUBLANES, LANES), jnp.float32),
            jax.ShapeDtypeStruct((3 * width + SUBLANES, LANES), jnp.float32),
            jax.ShapeDtypeStruct((2, width // 4, LANES), jnp.float32),
            jax.ShapeDtypeStruct((slots, 2, width, width), jnp.float32),
        ],
        in_specs=[smem, smem] + [vmem] * 12,
        out_specs=[vmem] * 4,
        scratch_shapes=[
            pltpu.VMEM((2, tile_r + 2 * half + SUBLANES, tile_c + 2 * half), jnp.float32),
            pltpu.VMEM((slots, 2, width, width), jnp.float32),
            pltpu.VMEM((2, slots * width, width), jnp.bfloat16),
            pltpu.VMEM((2, slots * width, width), jnp.bfloat16),
            pltpu.VMEM((2, width, slots * width), jnp.bfloat16),
            pltpu.VMEM((2, width, slots * width), jnp.bfloat16),
        ],
        compiler_params=pltpu.CompilerParams(vmem_limit_bytes=VMEM_LIMIT),
        cost_estimate=pl.CostEstimate(
            flops=3200000000, bytes_accessed=8000000, transcendentals=131072
        ),
    )(offsets, counts, probe, *map(in_vmem, staged), *map(in_vmem, blocks))


def finish_kernel(
    specimen, light, center, close, far, both, other, fresh, got, specimen_next, probe_next
):
    half = other.shape[2]
    row_place = lax.axis_index("row")
    col_place = lax.axis_index("col")
    row_odd = lax.rem(row_place, 2)
    col_odd = lax.rem(col_place, 2)
    far_at = row_place + 2 * row_odd - 1
    inside = (far_at >= 0) & (far_at < lax.axis_size("row"))
    for part in range(2):
        pair = both[part]
        rims = (
            jnp.where(col_odd == 0, other[part], pair),
            jnp.where(col_odd == 0, pair, other[part]),
        )
        for side, rim in enumerate(rims):
            at = slice(side * half, (side + 1) * half)
            k = 2 * side + part
            total = center[k] + close[k] + jnp.where(inside, far[k], 0.0) + rim
            specimen_next[part, :, at] = specimen[part, :, at] + total / light[:, at]
        mine, theirs = fresh[part], got[part]
        probe_next[part, :, :LANES] = jnp.where(row_odd == 0, mine, theirs)
        probe_next[part, :, LANES:] = jnp.where(row_odd == 0, theirs, mine)


def finish(specimen, probe, *values):
    vmem = pl.BlockSpec(memory_space=pltpu.VMEM)
    return pl.pallas_call(
        finish_kernel,
        out_shape=[
            jax.ShapeDtypeStruct(specimen.shape, jnp.float32),
            jax.ShapeDtypeStruct(probe.shape, jnp.float32),
        ],
        in_specs=[vmem] * (1 + len(values)),
        out_specs=[vmem] * 2,
        compiler_params=pltpu.CompilerParams(vmem_limit_bytes=VMEM_LIMIT),
        cost_estimate=pl.CostEstimate(flops=1000000, bytes_accessed=3000000, transcendentals=0),
    )(*map(in_vmem, (specimen, *values)))


def in_hbm(value):
    return pltpu.with_memory_space_constraint(value, pltpu.HBM)


def in_vmem(value):
    return pltpu.with_memory_space_constraint(value, pltpu.VMEM)


def fold_kernel(kept, got, own, across, beside, diagonal):
    layers = 3
    size = (own.shape[0] - SUBLANES) // layers
    here = 2 * lax.rem(lax.axis_index("row") // 2, 2) + lax.rem(lax.axis_index("col"), 2)
    total = kept[4 * layers * size :] + got[4 * layers * size :]
    for flip, out in enumerate((own, beside, across, diagonal)):
        row = 2 * (here // 2) + lax.rem(here, 2)
        row = (row // 2 + flip // 2) % 2 * 2 + (row % 2 + flip % 2) % 2
        for layer in range(layers):
            first = pl.multiple_of((4 * layer + row) * size, SUBLANES)
            at = pl.ds(first, size)
            out[layer * size : (layer + 1) * size] = kept[at] + got[at]
        out[layers * size :] = total


def fold(kept, got):
    vmem = pl.BlockSpec(memory_space=pltpu.VMEM)
    rows = (kept.shape[0] - SUBLANES) // 4 + SUBLANES
    return pl.pallas_call(
        fold_kernel,
        out_shape=[jax.ShapeDtypeStruct((rows, LANES), jnp.float32)] * 4,
        in_specs=[vmem] * 2,
        out_specs=[vmem] * 4,
        compiler_params=pltpu.CompilerParams(vmem_limit_bytes=VMEM_LIMIT),
        cost_estimate=pl.CostEstimate(flops=100000, bytes_accessed=400000, transcendentals=0),
    )(in_vmem(kept), in_vmem(got))


def place(offsets, probe, delta, tile_r, tile_c):
    width = probe.shape[1]
    half = width // 2
    smem = pl.BlockSpec(memory_space=pltpu.SMEM)
    vmem = pl.BlockSpec(memory_space=pltpu.VMEM)
    block = jax.ShapeDtypeStruct((4, tile_r, half), jnp.float32)
    return pl.pallas_call(
        place_kernel,
        out_shape=[block, block, jax.ShapeDtypeStruct((16, tile_r, half), jnp.float32)],
        in_specs=[smem, vmem, vmem],
        out_specs=[vmem] * 3,
        scratch_shapes=[
            pltpu.VMEM((2, tile_r + 2 * half + SUBLANES, tile_c + 2 * half), jnp.float32),
        ],
        compiler_params=pltpu.CompilerParams(vmem_limit_bytes=VMEM_LIMIT),
        cost_estimate=pl.CostEstimate(flops=4000000, bytes_accessed=4000000, transcendentals=0),
    )(offsets, probe, delta)


def exchange(value, axis, count, bit):
    return lax.ppermute(value, axis, [(i, i ^ bit) for i in range(count)])


def shards(specimen, probe_field, scan_offsets, live_counts, magnitudes):
    rows, cols = lax.axis_size("row"), lax.axis_size("col")
    width = probe_field.shape[1]
    half = width // 2
    tile_r, tile_c = specimen.shape[1:]
    row_place = lax.axis_index("row")
    col_place = lax.axis_index("col")
    row_odd = row_place % 2
    col_odd = col_place % 2
    pairs = [(i, i ^ 1) for i in range(cols)]
    others = [(i, i + 1) for i in range(1, cols - 1, 2)] + [(i + 1, i) for i in range(1, cols - 1, 2)]
    toward = [(i, i + 2) for i in range(1, rows - 2, 2)] + [(i, i - 2) for i in range(2, rows, 2)]
    toward += [(rows - 1, rows - 2), (0, 1)]
    onward_pairs = [(target, source) for source, target in toward]

    tie = lax.optimization_barrier

    def core(values):
        return [exchange(value, "row", rows, 1) for value in values]

    low, high = specimen[:, :, :half], specimen[:, :, tile_c - half :]
    pair_rim = lax.ppermute(jnp.where(col_odd == 0, high, low), "col", pairs)
    other_rim = lax.ppermute(jnp.where(col_odd == 0, low, high), "col", others)
    late, pair_rim = tie((magnitudes[0, 0], pair_rim))
    staged = stage(late)
    beyond = [lax.ppermute(block, "row", toward) for block in (specimen, pair_rim)]
    other_rim, staged, beyond = tie((other_rim, staged, beyond))
    own = [specimen, pair_rim, other_rim]
    beyond += [lax.ppermute(other_rim, "row", toward)]
    probe_late, other_rim = tie((probe_field, other_rim))
    light = lighting(scan_offsets, live_counts, probe_late, tile_r, tile_c)
    beyond[2], light = tie((beyond[2], light))
    kept, given, own_probe, delta = exit_update(
        scan_offsets, live_counts, probe_field, staged, own + core(own) + core(beyond)
    )

    def pick(condition, first, second):
        return jnp.where(condition, first, second)

    square = [
        (r * cols + c, (r ^ 2) * cols + (c ^ 1)) for r in range(rows) for c in range(cols)
    ]

    def all_three(across, beside, diagonal):
        diagonal = lax.ppermute(diagonal, ("row", "col"), square)
        return exchange(across, "row", rows, 2), exchange(beside, "col", cols, 1), diagonal

    got = exchange(given, "row", rows, 1)
    center_mid, center_rim, packet = place(scan_offsets, probe_field, delta, tile_r, tile_c)
    got, packet = tie((got, packet))
    packet = exchange(packet, "row", rows, 1)
    value, across, beside, diagonal = fold(kept, got)
    beyond_rim = lax.ppermute(packet[:4], "row", onward_pairs)
    beyond_mid = lax.ppermute(packet[4:8], "row", onward_pairs)
    across, beside, diagonal = all_three(across, beside, diagonal)
    value = (value + across) + (beside + diagonal)
    value, beyond_rim = tie((value, beyond_rim))
    inside = (row_place + 2 * row_odd - 1 >= 0) & (row_place + 2 * row_odd - 1 < rows)
    rim = center_rim + packet[8:12] + pick(inside, beyond_rim, 0.0)
    pair_part = rim[:2]
    other_part = lax.ppermute(rim[2:], "col", others)
    filled = jnp.concatenate([value, jnp.zeros((64, LANES), jnp.float32)])
    value = value + exchange(filled, "col", cols, 2)[: value.shape[0]]
    value, beyond_mid = tie((value, beyond_mid))
    for bit in (1 << k for k in range(2, cols.bit_length() - 1)):
        value = value + exchange(value, "col", cols, 2 * bit - 2)
    for bit in (1 << k for k in range(2, rows.bit_length() - 1)):
        value = value + exchange(value, "row", rows, bit)
    value, other_part, pair_part = tie((value, other_part, pair_part))
    size = own_probe.shape[1]
    real, imag, weight, total = (value[k * size : (k + 1) * size] for k in range(4))
    update = jnp.stack([real, imag]) / (weight + probe_damping * (total[:1] / (width * width)))
    fresh = own_probe + update
    size = fresh.size // LANES
    both = jnp.concatenate([fresh.reshape(size, LANES), pair_part.reshape(-1, LANES)])
    across, both, diagonal = all_three(fresh, both, fresh)
    beside = both[:size].reshape(fresh.shape)
    pair_part = both[size:].reshape(pair_part.shape)

    def ordered(place_here, one, other):
        return pick(
            place_here == 0,
            jnp.concatenate([one, other], 1),
            jnp.concatenate([other, one], 1),
        )

    fresh = ordered(
        (row_place // 2) % 2, ordered(col_odd, fresh, beside), ordered(col_odd, across, diagonal)
    )
    got = exchange(fresh, "row", rows, 1)
    return finish(
        specimen, probe_field, light, center_mid, packet[12:], beyond_mid,
        pair_part, other_part, fresh, got,
    )


def solution(mesh):
    return jax.shard_map(
        shards,
        mesh=mesh,
        in_specs=(P(None, "row", "col"), P(), P(), P(), P("row", "col", None, None, None)),
        out_specs=(P(None, "row", "col"), P()),
        check_vma=False,
    )
```

```python
import functools
import math

import jax
import jax.numpy as jnp
import ml_dtypes
import numpy as np
from jax import lax
from jax.experimental import pallas as pl
from jax.experimental.pallas import tpu as pltpu
from jax.sharding import PartitionSpec as P

modulus_floor = 0.25
object_damping = 0.1
probe_damping = 0.1
LANES = 128
SUBLANES = 8
VMEM_LIMIT = 20 * 1024 * 1024


def dft_tables(width):
    half = width // 2
    counter = np.arange(half)
    tables = []
    for odd in range(2):
        phase = counter[:, None] * (2 * counter[None, :] + odd) % width
        angle = phase * (2.0 * math.pi / width)
        real, imag = np.cos(angle) / math.sqrt(width), -np.sin(angle) / math.sqrt(width)
        tables.append(np.block([[real, imag], [-imag, real]]))
    tables = np.stack(tables + [table.T for table in tables])
    high = tables.astype(ml_dtypes.bfloat16)
    low = (tables - high.astype(np.float64)).astype(ml_dtypes.bfloat16)
    return np.stack([high, low], 1)


def halves(value):
    high = value.astype(jnp.bfloat16)
    return high, (value - high.astype(jnp.float32)).astype(jnp.bfloat16)


def product(left, right):
    dot = functools.partial(jnp.dot, preferred_element_type=jnp.float32)
    return dot(left[0], right[0]) + (dot(left[1], right[0]) + dot(left[0], right[1]))


def keep(ref, rows, lanes, value):
    for place, half in enumerate(halves(value)):
        ref[place, rows, lanes] = half


def product_of(left, right):
    return product((left[0], left[1]), (right[0], right[1]))


def split_start(start, step, last):
    aligned = jnp.minimum(start // step, last // step) * step
    return pl.multiple_of(aligned, step), start - aligned


def lane_groups(value):
    return [value[..., at : at + LANES] for at in range(0, value.shape[-1], LANES)]


def cut(value, row_shift, lane_shift):
    rows, lanes = value.shape
    value = value.reshape(rows // SUBLANES, SUBLANES, lanes)
    lane_turn = lax.rem(LANES - lane_shift, LANES)
    row_turn = lax.rem(SUBLANES - row_shift, SUBLANES)
    shape = (rows // SUBLANES, SUBLANES, LANES)
    keep_lane = lax.broadcasted_iota(jnp.int32, shape, 2) < LANES - lane_shift
    keep_row = lax.broadcasted_iota(jnp.int32, shape, 1)[1:] < SUBLANES - row_shift
    turned = [pltpu.roll(group, lane_turn, 2) for group in lane_groups(value)]
    parts = []
    for first, second in zip(turned[:-1], turned[1:]):
        part = pltpu.roll(jnp.where(keep_lane, first, second), row_turn, 1)
        part = jnp.where(keep_row, part[:-1], part[1:])
        parts.append(part.reshape(rows - SUBLANES, LANES))
    return jnp.concatenate(parts, 1)


def spread(value, row_shift, lane_shift):
    rows, lanes = value.shape
    value = value.reshape(rows // SUBLANES, SUBLANES, lanes)
    shape = (rows // SUBLANES + 1, SUBLANES, LANES)
    lane_turn = lax.rem(lane_shift, LANES)
    take_lane = lax.broadcasted_iota(jnp.int32, shape, 2) < lane_shift
    take_row = lax.broadcasted_iota(jnp.int32, shape, 1) < row_shift
    blank_row = jnp.zeros((1, SUBLANES, LANES), value.dtype)
    turned = []
    for group in lane_groups(value):
        group = pltpu.roll(group, row_shift, 1)
        group = jnp.where(
            take_row,
            jnp.concatenate([blank_row, group], 0),
            jnp.concatenate([group, blank_row], 0),
        )
        turned.append(pltpu.roll(group, lane_turn, 2))
    blank = jnp.zeros(shape, value.dtype)
    parts = [
        jnp.where(take_lane, first, second).reshape(rows + SUBLANES, LANES)
        for first, second in zip([blank] + turned, turned + [blank])
    ]
    return jnp.concatenate(parts, 1)


def lighting_kernel(offsets, counts, probe, out, pad):
    rows, cols, slots = offsets.shape[:3]
    tile_r, tile_c = out.shape
    width = probe.shape[1]
    half = width // 2
    row_place = lax.axis_index("row")
    col_place = lax.axis_index("col")
    power = probe[0] * probe[0] + probe[1] * probe[1]
    pad[...] = jnp.zeros_like(pad)
    pad[tile_r : tile_r + width, tile_c : tile_c + width] = power
    out[...] = jnp.full(out.shape, object_damping * jnp.max(power))
    wide = tile_c + LANES
    for row_step in (-1, 0, 1):
        for col_step in (-1, 0, 1):
            row, col = row_place + row_step, col_place + col_step
            inside = (row >= 0) & (row < rows) & (col >= 0) & (col < cols)
            row_at = jnp.clip(row, 0, rows - 1)
            col_at = jnp.clip(col, 0, cols - 1)
            for slot in range(slots):
                top = offsets[row_at, col_at, slot, 0] + row_step * tile_r
                left = offsets[row_at, col_at, slot, 1] + col_step * tile_c

                @pl.when(
                    inside
                    & (slot < counts[row_at, col_at])
                    & (left > -width)
                    & (left < tile_c)
                )
                def _():
                    row, row_shift = split_start(tile_r - top, SUBLANES, tile_r + width)
                    lane, lane_shift = split_start(tile_c - left, LANES, pad.shape[1] - wide)
                    part = pad[pl.ds(row, tile_r + SUBLANES), pl.ds(lane, wide)]
                    out[...] += cut(part, row_shift, lane_shift)


def lighting(offsets, counts, probe, tile_r, tile_c):
    width = probe.shape[1]
    smem = pl.BlockSpec(memory_space=pltpu.SMEM)
    vmem = pl.BlockSpec(memory_space=pltpu.VMEM)
    return pl.pallas_call(
        lighting_kernel,
        out_shape=jax.ShapeDtypeStruct((tile_r, tile_c), jnp.float32),
        in_specs=[smem, smem, vmem],
        out_specs=vmem,
        scratch_shapes=[
            pltpu.VMEM((2 * tile_r + width + SUBLANES, 2 * tile_c + width), jnp.float32)
        ],
        compiler_params=pltpu.CompilerParams(vmem_limit_bytes=VMEM_LIMIT),
        cost_estimate=pl.CostEstimate(flops=40000000, bytes_accessed=8000000, transcendentals=0),
    )(offsets, counts, probe)


def patch_block(offsets, row_place, col_place, slot, half, tile_r, width):
    row, row_shift = split_start(offsets[row_place, col_place, slot, 0] + half, SUBLANES, tile_r)
    lane, lane_shift = split_start(
        offsets[row_place, col_place, slot, 1] + half, LANES, 2 * half - LANES
    )
    return (pl.ds(row, width + SUBLANES), pl.ds(lane, width + LANES)), row_shift, lane_shift


def delta_kernel(
    offsets, counts, probe, magnitudes, tables,
    own, pair_rim, other_rim, near, near_pair, near_other, far, far_pair, far_other,
    kept, given, own_probe, delta, ext, patches, tall_even, tall_odd, wide_even, wide_odd,
):
    slots, width = magnitudes.shape[0], magnitudes.shape[1]
    half = width // 2
    tile_r, tile_c = own.shape[1:]
    row_place = lax.axis_index("row")
    col_place = lax.axis_index("col")
    row_odd = lax.rem(row_place, 2)
    col_odd = lax.rem(col_place, 2)
    near_row = pl.multiple_of((1 - row_odd) * (tile_r + half), half)
    far_row = pl.multiple_of(row_odd * (tile_r + half), half)
    pair_col = pl.multiple_of((1 - col_odd) * (tile_c + half), half)
    other_col = pl.multiple_of(col_odd * (tile_c + half), half)
    far_at = row_place + 2 * row_odd - 1
    inside = (far_at >= 0) & (far_at < lax.axis_size("row"))
    strips = (
        (half, True, own, pair_rim, other_rim),
        (near_row, True, near, near_pair, near_other),
        (far_row, inside, far, far_pair, far_other),
    )
    for part in range(2):
        for row, valid, *blocks in strips:
            at = pl.ds(row, tile_r)
            mid, pair, other = (
                block[part] if valid is True else jnp.where(valid, block[part], 0.0)
                for block in blocks
            )
            ext[part, at, half : half + tile_c] = mid
            ext[part, at, pl.ds(pair_col, half)] = pair
            ext[part, at, pl.ds(other_col, half)] = other
    live_count = counts[row_place, col_place]
    probe_real, probe_imag = probe[0], probe[1]
    right_even, right_odd, left_even, left_odd = (tables.at[k] for k in range(4))
    low, high = slice(0, half), slice(half, width)
    for slot in range(slots):
        block, row_shift, lane_shift = patch_block(
            offsets, row_place, col_place, slot, half, tile_r, width
        )
        for part in range(2):
            patches[slot, part] = cut(ext[part, *block], row_shift, lane_shift)
        patch_real, patch_imag = patches[slot, 0], patches[slot, 1]
        at = slice(slot * width, (slot + 1) * width)
        for part, wave in (
            (low, probe_real * patch_real - probe_imag * patch_imag),
            (high, probe_real * patch_imag + probe_imag * patch_real),
        ):
            keep(tall_even, at, part, wave[:, low] + wave[:, high])
            keep(tall_odd, at, part, wave[:, low] - wave[:, high])
    inner = (product_of(tall_even, right_even), product_of(tall_odd, right_odd))
    for slot in range(slots):
        top = slice(slot * width, slot * width + half)
        bottom = slice(slot * width + half, (slot + 1) * width)
        for odd in range(2):
            at = slice(slot * width + odd * half, slot * width + (odd + 1) * half)
            for part in (low, high):
                upper, lower = inner[odd][top, part], inner[odd][bottom, part]
                keep(wide_even, part, at, upper + lower)
                keep(wide_odd, part, at, upper - lower)
    outer = (product_of(left_even, wide_even), product_of(left_odd, wide_odd))
    for slot in range(slots):
        lanes = slice(slot * width, (slot + 1) * width)
        for odd in range(2):
            far_real, far_imag = outer[odd][low, lanes], outer[odd][high, lanes]
            inverse = jnp.minimum(
                lax.rsqrt(far_real * far_real + far_imag * far_imag), 1.0 / modulus_floor
            )
            factor = magnitudes[slot, odd * half : (odd + 1) * half] * inverse - 1.0
            at = slice(slot * width + odd * half, slot * width + (odd + 1) * half)
            for part, back in ((low, far_real * factor), (high, far_imag * factor)):
                keep(tall_even, at, part, back[:, low])
                keep(tall_odd, at, part, back[:, high])
    inner = (product_of(tall_even, left_even), product_of(tall_odd, left_odd))
    for slot in range(slots):
        for odd, ref in enumerate((wide_even, wide_odd)):
            at = slice(slot * width + odd * half, slot * width + (odd + 1) * half)
            for part in (low, high):
                one, other = inner[0][at, part], inner[1][at, part]
                keep(ref, part, slice(slot * width, slot * width + half), one + other)
                keep(ref, part, slice(slot * width + half, (slot + 1) * width), one - other)
    outer = (product_of(right_even, wide_even), product_of(right_odd, wide_odd))
    sums = [jnp.zeros((width, width), jnp.float32)] * 3
    for slot in range(slots):
        live = jnp.where(slot < live_count, 1.0, 0.0)
        lanes = slice(slot * width, (slot + 1) * width)
        for part, rows in enumerate((low, high)):
            one, other = outer[0][rows, lanes], outer[1][rows, lanes]
            delta[slot, part, low] = (one + other) * live
            delta[slot, part, high] = (one - other) * live
        delta_real, delta_imag = delta[slot, 0], delta[slot, 1]
        patch_real, patch_imag = patches[slot, 0], patches[slot, 1]
        sums = [
            sums[0] + (patch_real * delta_real + patch_imag * delta_imag),
            sums[1] + (patch_real * delta_imag - patch_imag * delta_real),
            sums[2] + live * (patch_real * patch_real + patch_imag * patch_imag),
        ]
    even = row_odd == 0
    for layer in range(3):
        one, other = lane_groups(sums[layer])
        kept[layer * width : (layer + 1) * width] = jnp.where(even, one, other)
        given[layer * width : (layer + 1) * width] = jnp.where(even, other, one)
    total = jnp.full((SUBLANES, LANES), jnp.sum(sums[2]))
    kept[3 * width :] = total
    given[3 * width :] = total
    size = own_probe.shape[1]
    row = pl.multiple_of(lax.rem(row_place // 2, 2) * (2 * size) + col_odd * size, size)
    for part in range(2):
        one, other = lane_groups(probe[part, pl.ds(row, size), :])
        own_probe[part] = jnp.where(even, one, other)


def place_kernel(
    offsets, probe, delta, *blocks_and_ext
):
    center_mid, center_rim, packet, ext = blocks_and_ext
    slots, width = delta.shape[0], delta.shape[2]
    half = width // 2
    tile_r = center_mid.shape[1]
    tile_c = ext.shape[2] - 2 * half
    row_place = lax.axis_index("row")
    col_place = lax.axis_index("col")
    row_odd = lax.rem(row_place, 2)
    col_odd = lax.rem(col_place, 2)
    ext[...] = jnp.zeros_like(ext)
    probe_real, probe_imag = probe[0], probe[1]
    for slot in range(slots):
        real, imag = delta[slot, 0], delta[slot, 1]
        block, row_shift, lane_shift = patch_block(
            offsets, row_place, col_place, slot, half, tile_r, width
        )
        for part, grad in enumerate(
            (probe_real * real + probe_imag * imag, probe_real * imag - probe_imag * real)
        ):
            ext[part, *block] += spread(grad, row_shift, lane_shift)
    near_row = pl.multiple_of((1 - row_odd) * (tile_r + half), half)
    far_row = pl.multiple_of(row_odd * (tile_r + half), half)
    pair_col = pl.multiple_of((1 - col_odd) * (tile_c + half), half)
    other_col = pl.multiple_of(col_odd * (tile_c + half), half)
    middle = tile_c // 2
    for row, rim, mid in (
        (half, center_rim, center_mid),
        (far_row, packet.at[0:4], packet.at[4:8]),
        (near_row, packet.at[8:12], packet.at[12:16]),
    ):
        at = pl.ds(row, tile_r)
        mid[0:2] = ext[:, at, half : half + middle]
        mid[2:4] = ext[:, at, half + middle : half + tile_c]
        rim[0:2] = ext[:, at, pl.ds(pair_col, half)]
        rim[2:4] = ext[:, at, pl.ds(other_col, half)]


def stage_kernel(magnitudes, tables, ordered, held, measured, arrived):
    slots, width = magnitudes.shape[:2]
    copies = [
        pltpu.make_async_copy(tables, held, arrived.at[0]),
        pltpu.make_async_copy(magnitudes, measured, arrived.at[1]),
    ]
    for copy in copies:
        copy.start()
    line = lax.broadcasted_iota(jnp.int32, (width, width), 0)
    place = lax.broadcasted_iota(jnp.int32, (width, width), 1)

    def chosen(here, there):
        source = jnp.where(here < width // 2, 2 * here, 2 * here - (width - 1))
        return jnp.where(source == there, 1.0, 0.0).astype(jnp.bfloat16)

    by_row, by_lane = chosen(line, place), chosen(place, line)
    copies[1].wait()
    for slot in range(slots):
        rest = measured[slot]
        total = jnp.zeros((width, width), jnp.float32)
        for _ in range(3):
            piece = rest.astype(jnp.bfloat16)
            rest = rest - piece.astype(jnp.float32)
            piece = jnp.dot(by_row, piece, preferred_element_type=jnp.float32)
            total += jnp.dot(
                piece.astype(jnp.bfloat16), by_lane, preferred_element_type=jnp.float32
            )
        ordered[slot] = total
    copies[0].wait()


def stage(magnitudes):
    width = magnitudes.shape[-1]
    hbm = pl.BlockSpec(memory_space=pltpu.HBM)
    vmem = pl.BlockSpec(memory_space=pltpu.VMEM)
    return pl.pallas_call(
        stage_kernel,
        out_shape=[
            jax.ShapeDtypeStruct(magnitudes.shape, jnp.float32),
            jax.ShapeDtypeStruct((4, 2, width, width), jnp.bfloat16),
        ],
        in_specs=[hbm] * 2,
        out_specs=[vmem] * 2,
        scratch_shapes=[
            pltpu.VMEM(magnitudes.shape, jnp.float32),
            pltpu.SemaphoreType.DMA((2,)),
        ],
        compiler_params=pltpu.CompilerParams(vmem_limit_bytes=VMEM_LIMIT),
        cost_estimate=pl.CostEstimate(flops=400000000, bytes_accessed=3000000, transcendentals=0),
    )(in_hbm(magnitudes), in_hbm(jnp.asarray(dft_tables(width))))


def exit_update(offsets, counts, probe, staged, blocks):
    slots, width = staged[0].shape[:2]
    own = blocks[0]
    half = width // 2
    tile_r, tile_c = own.shape[1:]
    smem = pl.BlockSpec(memory_space=pltpu.SMEM)
    vmem = pl.BlockSpec(memory_space=pltpu.VMEM)
    return pl.pallas_call(
        delta_kernel,
        out_shape=[
            jax.ShapeDtypeStruct((3 * width + SUBLANES, LANES), jnp.float32),
            jax.ShapeDtypeStruct((3 * width + SUBLANES, LANES), jnp.float32),
            jax.ShapeDtypeStruct((2, width // 4, LANES), jnp.float32),
            jax.ShapeDtypeStruct((slots, 2, width, width), jnp.float32),
        ],
        in_specs=[smem, smem] + [vmem] * 12,
        out_specs=[vmem] * 4,
        scratch_shapes=[
            pltpu.VMEM((2, tile_r + 2 * half + SUBLANES, tile_c + 2 * half), jnp.float32),
            pltpu.VMEM((slots, 2, width, width), jnp.float32),
            pltpu.VMEM((2, slots * width, width), jnp.bfloat16),
            pltpu.VMEM((2, slots * width, width), jnp.bfloat16),
            pltpu.VMEM((2, width, slots * width), jnp.bfloat16),
            pltpu.VMEM((2, width, slots * width), jnp.bfloat16),
        ],
        compiler_params=pltpu.CompilerParams(vmem_limit_bytes=VMEM_LIMIT),
        cost_estimate=pl.CostEstimate(
            flops=3200000000, bytes_accessed=8000000, transcendentals=131072
        ),
    )(offsets, counts, probe, *map(in_vmem, staged), *map(in_vmem, blocks))


def finish_kernel(
    specimen, light, center, close, far, both, other, fresh, got, specimen_next, probe_next
):
    half = other.shape[2]
    row_place = lax.axis_index("row")
    col_place = lax.axis_index("col")
    row_odd = lax.rem(row_place, 2)
    col_odd = lax.rem(col_place, 2)
    far_at = row_place + 2 * row_odd - 1
    inside = (far_at >= 0) & (far_at < lax.axis_size("row"))
    other_at = col_place + 2 * col_odd - 1
    beside = (other_at >= 0) & (other_at < lax.axis_size("col"))
    for part in range(2):
        pair, apart = both[part], jnp.where(beside, other[part], 0.0)
        rims = (
            jnp.where(col_odd == 0, apart, pair),
            jnp.where(col_odd == 0, pair, apart),
        )
        for side, rim in enumerate(rims):
            at = slice(side * half, (side + 1) * half)
            k = 2 * side + part
            total = center[k] + close[k] + jnp.where(inside, far[k], 0.0) + rim
            specimen_next[part, :, at] = specimen[part, :, at] + total / light[:, at]
        mine, theirs = fresh[part], got[part]
        probe_next[part, :, :LANES] = jnp.where(row_odd == 0, mine, theirs)
        probe_next[part, :, LANES:] = jnp.where(row_odd == 0, theirs, mine)


def finish(specimen, probe, *values):
    vmem = pl.BlockSpec(memory_space=pltpu.VMEM)
    return pl.pallas_call(
        finish_kernel,
        out_shape=[
            jax.ShapeDtypeStruct(specimen.shape, jnp.float32),
            jax.ShapeDtypeStruct(probe.shape, jnp.float32),
        ],
        in_specs=[vmem] * (1 + len(values)),
        out_specs=[vmem] * 2,
        compiler_params=pltpu.CompilerParams(vmem_limit_bytes=VMEM_LIMIT),
        cost_estimate=pl.CostEstimate(flops=1000000, bytes_accessed=3000000, transcendentals=0),
    )(*map(in_vmem, (specimen, *values)))


def in_hbm(value):
    return pltpu.with_memory_space_constraint(value, pltpu.HBM)


def in_vmem(value):
    return pltpu.with_memory_space_constraint(value, pltpu.VMEM)


def fold_kernel(kept, got, own, across, beside, diagonal):
    layers = 3
    size = (own.shape[0] - SUBLANES) // layers
    here = 2 * lax.rem(lax.axis_index("row") // 2, 2) + lax.rem(lax.axis_index("col"), 2)
    total = kept[4 * layers * size :] + got[4 * layers * size :]
    for flip, out in enumerate((own, beside, across, diagonal)):
        row = 2 * (here // 2) + lax.rem(here, 2)
        row = (row // 2 + flip // 2) % 2 * 2 + (row % 2 + flip % 2) % 2
        for layer in range(layers):
            first = pl.multiple_of((4 * layer + row) * size, SUBLANES)
            at = pl.ds(first, size)
            out[layer * size : (layer + 1) * size] = kept[at] + got[at]
        out[layers * size :] = total


def fold(kept, got):
    vmem = pl.BlockSpec(memory_space=pltpu.VMEM)
    rows = (kept.shape[0] - SUBLANES) // 4 + SUBLANES
    return pl.pallas_call(
        fold_kernel,
        out_shape=[jax.ShapeDtypeStruct((rows, LANES), jnp.float32)] * 4,
        in_specs=[vmem] * 2,
        out_specs=[vmem] * 4,
        compiler_params=pltpu.CompilerParams(vmem_limit_bytes=VMEM_LIMIT),
        cost_estimate=pl.CostEstimate(flops=100000, bytes_accessed=400000, transcendentals=0),
    )(in_vmem(kept), in_vmem(got))


def place(offsets, probe, delta, tile_r, tile_c):
    width = probe.shape[1]
    half = width // 2
    smem = pl.BlockSpec(memory_space=pltpu.SMEM)
    vmem = pl.BlockSpec(memory_space=pltpu.VMEM)
    block = jax.ShapeDtypeStruct((4, tile_r, half), jnp.float32)
    return pl.pallas_call(
        place_kernel,
        out_shape=[block, block, jax.ShapeDtypeStruct((16, tile_r, half), jnp.float32)],
        in_specs=[smem, vmem, vmem],
        out_specs=[vmem] * 3,
        scratch_shapes=[
            pltpu.VMEM((2, tile_r + 2 * half + SUBLANES, tile_c + 2 * half), jnp.float32),
        ],
        compiler_params=pltpu.CompilerParams(vmem_limit_bytes=VMEM_LIMIT),
        cost_estimate=pl.CostEstimate(flops=4000000, bytes_accessed=4000000, transcendentals=0),
    )(offsets, probe, delta)


def exchange(value, axis, count, bit):
    return lax.ppermute(value, axis, [(i, i ^ bit) for i in range(count)])


def shards(specimen, probe_field, scan_offsets, live_counts, magnitudes):
    rows, cols = lax.axis_size("row"), lax.axis_size("col")
    width = probe_field.shape[1]
    half = width // 2
    tile_r, tile_c = specimen.shape[1:]
    row_place = lax.axis_index("row")
    col_place = lax.axis_index("col")
    row_odd = row_place % 2
    col_odd = col_place % 2
    pairs = [(i, i ^ 1) for i in range(cols)]
    others = [(i, i + 1) for i in range(1, cols - 1, 2)] + [(i + 1, i) for i in range(1, cols - 1, 2)]
    toward = [(i, i + 2) for i in range(1, rows - 2, 2)] + [(i, i - 2) for i in range(2, rows, 2)]
    toward += [(rows - 1, rows - 2), (0, 1)]
    onward_pairs = [(target, source) for source, target in toward]

    tie = lax.optimization_barrier

    def core(values):
        return [exchange(value, "row", rows, 1) for value in values]

    low, high = specimen[:, :, :half], specimen[:, :, tile_c - half :]
    pair_rim = lax.ppermute(jnp.where(col_odd == 0, high, low), "col", pairs)
    other_rim = lax.ppermute(jnp.where(col_odd == 0, low, high), "col", others)
    late, pair_rim = tie((magnitudes[0, 0], pair_rim))
    staged = stage(late)
    beyond = [lax.ppermute(block, "row", toward) for block in (specimen, pair_rim)]
    other_rim, staged, beyond = tie((other_rim, staged, beyond))
    own = [specimen, pair_rim, other_rim]
    beyond += [lax.ppermute(other_rim, "row", toward)]
    probe_late, other_rim = tie((probe_field, other_rim))
    light = lighting(scan_offsets, live_counts, probe_late, tile_r, tile_c)
    beyond[2], light = tie((beyond[2], light))
    kept, given, own_probe, delta = exit_update(
        scan_offsets, live_counts, probe_field, staged, own + core(own) + core(beyond)
    )

    def pick(condition, first, second):
        return jnp.where(condition, first, second)

    square = [
        (r * cols + c, (r ^ 2) * cols + (c ^ 1)) for r in range(rows) for c in range(cols)
    ]

    def all_three(across, beside, diagonal):
        diagonal = lax.ppermute(diagonal, ("row", "col"), square)
        return exchange(across, "row", rows, 2), exchange(beside, "col", cols, 1), diagonal

    got = exchange(given, "row", rows, 1)
    center_mid, center_rim, packet = place(scan_offsets, probe_field, delta, tile_r, tile_c)
    got, packet = tie((got, packet))
    packet = exchange(packet, "row", rows, 1)
    value, across, beside, diagonal = fold(kept, got)
    beyond_rim = lax.ppermute(packet[:4], "row", onward_pairs)
    beyond_mid = lax.ppermute(packet[4:8], "row", onward_pairs)
    across, beside, diagonal = all_three(across, beside, diagonal)
    value = (value + across) + (beside + diagonal)
    value, beyond_rim = tie((value, beyond_rim))
    inside = (row_place + 2 * row_odd - 1 >= 0) & (row_place + 2 * row_odd - 1 < rows)
    rim = center_rim + packet[8:12] + pick(inside, beyond_rim, 0.0)
    pair_part = rim[:2]
    other_part = lax.ppermute(rim[2:], "col", others + [(0, cols - 1), (cols - 1, 0)])
    value = value + exchange(value, "col", cols, 2)
    for bit in (1 << k for k in range(2, cols.bit_length() - 1)):
        value = value + exchange(value, "col", cols, 2 * bit - 2)
    for bit in (1 << k for k in range(2, rows.bit_length() - 1)):
        value = value + exchange(value, "row", rows, bit)
    value, other_part, pair_part, beyond_mid = tie(
        (value, other_part, pair_part, beyond_mid)
    )
    size = own_probe.shape[1]
    real, imag, weight, total = (value[k * size : (k + 1) * size] for k in range(4))
    update = jnp.stack([real, imag]) / (weight + probe_damping * (total[:1] / (width * width)))
    fresh = own_probe + update
    size = fresh.size // LANES
    both = jnp.concatenate([fresh.reshape(size, LANES), pair_part.reshape(-1, LANES)])
    across, both, diagonal = all_three(fresh, both, fresh)
    beside = both[:size].reshape(fresh.shape)
    pair_part = both[size:].reshape(pair_part.shape)

    def ordered(place_here, one, other):
        return pick(
            place_here == 0,
            jnp.concatenate([one, other], 1),
            jnp.concatenate([other, one], 1),
        )

    fresh = ordered(
        (row_place // 2) % 2, ordered(col_odd, fresh, beside), ordered(col_odd, across, diagonal)
    )
    got = exchange(fresh, "row", rows, 1)
    return finish(
        specimen, probe_field, light, center_mid, packet[12:], beyond_mid,
        pair_part, other_part, fresh, got,
    )


def solution(mesh):
    return jax.shard_map(
        shards,
        mesh=mesh,
        in_specs=(P(None, "row", "col"), P(), P(), P(), P("row", "col", None, None, None)),
        out_specs=(P(None, "row", "col"), P()),
        check_vma=False,
    )
```

```python
import functools
import math

import jax
import jax.numpy as jnp
import ml_dtypes
import numpy as np
from jax import lax
from jax.experimental import pallas as pl
from jax.experimental.pallas import tpu as pltpu
from jax.sharding import PartitionSpec as P

modulus_floor = 0.25
object_damping = 0.1
probe_damping = 0.1
LANES = 128
SUBLANES = 8
VMEM_LIMIT = 20 * 1024 * 1024


def dft_tables(width):
    half = width // 2
    counter = np.arange(half)
    tables = []
    for odd in range(2):
        phase = counter[:, None] * (2 * counter[None, :] + odd) % width
        angle = phase * (2.0 * math.pi / width)
        real, imag = np.cos(angle) / math.sqrt(width), -np.sin(angle) / math.sqrt(width)
        tables.append(np.block([[real, imag], [-imag, real]]))
    tables = np.stack(tables + [table.T for table in tables])
    high = tables.astype(ml_dtypes.bfloat16)
    low = (tables - high.astype(np.float64)).astype(ml_dtypes.bfloat16)
    return np.stack([high, low], 1)


def halves(value):
    high = value.astype(jnp.bfloat16)
    return high, (value - high.astype(jnp.float32)).astype(jnp.bfloat16)


def product(left, right):
    dot = functools.partial(jnp.dot, preferred_element_type=jnp.float32)
    return dot(left[0], right[0]) + (dot(left[1], right[0]) + dot(left[0], right[1]))


def keep(ref, rows, lanes, value):
    for place, half in enumerate(halves(value)):
        ref[place, rows, lanes] = half


def product_of(left, right):
    return product((left[0], left[1]), (right[0], right[1]))


def split_start(start, step, last):
    aligned = jnp.minimum(start // step, last // step) * step
    return pl.multiple_of(aligned, step), start - aligned


def lane_groups(value):
    return [value[..., at : at + LANES] for at in range(0, value.shape[-1], LANES)]


def cut(value, row_shift, lane_shift):
    rows, lanes = value.shape
    value = value.reshape(rows // SUBLANES, SUBLANES, lanes)
    lane_turn = lax.rem(LANES - lane_shift, LANES)
    row_turn = lax.rem(SUBLANES - row_shift, SUBLANES)
    shape = (rows // SUBLANES, SUBLANES, LANES)
    keep_lane = lax.broadcasted_iota(jnp.int32, shape, 2) < LANES - lane_shift
    keep_row = lax.broadcasted_iota(jnp.int32, shape, 1)[1:] < SUBLANES - row_shift
    turned = [pltpu.roll(group, lane_turn, 2) for group in lane_groups(value)]
    parts = []
    for first, second in zip(turned[:-1], turned[1:]):
        part = pltpu.roll(jnp.where(keep_lane, first, second), row_turn, 1)
        part = jnp.where(keep_row, part[:-1], part[1:])
        parts.append(part.reshape(rows - SUBLANES, LANES))
    return jnp.concatenate(parts, 1)


def spread(value, row_shift, lane_shift):
    rows, lanes = value.shape
    value = value.reshape(rows // SUBLANES, SUBLANES, lanes)
    shape = (rows // SUBLANES + 1, SUBLANES, LANES)
    lane_turn = lax.rem(lane_shift, LANES)
    take_lane = lax.broadcasted_iota(jnp.int32, shape, 2) < lane_shift
    take_row = lax.broadcasted_iota(jnp.int32, shape, 1) < row_shift
    blank_row = jnp.zeros((1, SUBLANES, LANES), value.dtype)
    turned = []
    for group in lane_groups(value):
        group = pltpu.roll(group, row_shift, 1)
        group = jnp.where(
            take_row,
            jnp.concatenate([blank_row, group], 0),
            jnp.concatenate([group, blank_row], 0),
        )
        turned.append(pltpu.roll(group, lane_turn, 2))
    blank = jnp.zeros(shape, value.dtype)
    parts = [
        jnp.where(take_lane, first, second).reshape(rows + SUBLANES, LANES)
        for first, second in zip([blank] + turned, turned + [blank])
    ]
    return jnp.concatenate(parts, 1)


def lighting_kernel(offsets, counts, probe, out, pad):
    rows, cols, slots = offsets.shape[:3]
    tile_r, tile_c = out.shape
    width = probe.shape[1]
    half = width // 2
    row_place = lax.axis_index("row")
    col_place = lax.axis_index("col")
    power = probe[0] * probe[0] + probe[1] * probe[1]
    pad[...] = jnp.zeros_like(pad)
    pad[tile_r : tile_r + width, tile_c : tile_c + width] = power
    out[...] = jnp.full(out.shape, object_damping * jnp.max(power))
    wide = tile_c + LANES
    for row_step in (-1, 0, 1):
        for col_step in (-1, 0, 1):
            row, col = row_place + row_step, col_place + col_step
            inside = (row >= 0) & (row < rows) & (col >= 0) & (col < cols)
            row_at = jnp.clip(row, 0, rows - 1)
            col_at = jnp.clip(col, 0, cols - 1)
            for slot in range(slots):
                top = offsets[row_at, col_at, slot, 0] + row_step * tile_r
                left = offsets[row_at, col_at, slot, 1] + col_step * tile_c

                @pl.when(
                    inside
                    & (slot < counts[row_at, col_at])
                    & (left > -width)
                    & (left < tile_c)
                )
                def _():
                    row, row_shift = split_start(tile_r - top, SUBLANES, tile_r + width)
                    lane, lane_shift = split_start(tile_c - left, LANES, pad.shape[1] - wide)
                    part = pad[pl.ds(row, tile_r + SUBLANES), pl.ds(lane, wide)]
                    out[...] += cut(part, row_shift, lane_shift)


def lighting(offsets, counts, probe, tile_r, tile_c):
    width = probe.shape[1]
    smem = pl.BlockSpec(memory_space=pltpu.SMEM)
    vmem = pl.BlockSpec(memory_space=pltpu.VMEM)
    return pl.pallas_call(
        lighting_kernel,
        out_shape=jax.ShapeDtypeStruct((tile_r, tile_c), jnp.float32),
        in_specs=[smem, smem, vmem],
        out_specs=vmem,
        scratch_shapes=[
            pltpu.VMEM((2 * tile_r + width + SUBLANES, 2 * tile_c + width), jnp.float32)
        ],
        compiler_params=pltpu.CompilerParams(vmem_limit_bytes=VMEM_LIMIT),
        cost_estimate=pl.CostEstimate(flops=40000000, bytes_accessed=8000000, transcendentals=0),
    )(offsets, counts, probe)


def patch_block(offsets, row_place, col_place, slot, half, tile_r, width):
    row, row_shift = split_start(offsets[row_place, col_place, slot, 0] + half, SUBLANES, tile_r)
    lane, lane_shift = split_start(
        offsets[row_place, col_place, slot, 1] + half, LANES, 2 * half - LANES
    )
    return (pl.ds(row, width + SUBLANES), pl.ds(lane, width + LANES)), row_shift, lane_shift


def delta_kernel(
    offsets, counts, probe, magnitudes, tables,
    own, pair_rim, other_rim, near, near_pair, near_other, far, far_pair, far_other,
    kept, given, own_probe, delta, ext, patches, tall_even, tall_odd, wide_even, wide_odd,
):
    slots, width = magnitudes.shape[0], magnitudes.shape[1]
    half = width // 2
    tile_r, tile_c = own.shape[1:]
    row_place = lax.axis_index("row")
    col_place = lax.axis_index("col")
    row_odd = lax.rem(row_place, 2)
    col_odd = lax.rem(col_place, 2)
    near_row = pl.multiple_of((1 - row_odd) * (tile_r + half), half)
    far_row = pl.multiple_of(row_odd * (tile_r + half), half)
    pair_col = pl.multiple_of((1 - col_odd) * (tile_c + half), half)
    other_col = pl.multiple_of(col_odd * (tile_c + half), half)
    far_at = row_place + 2 * row_odd - 1
    inside = (far_at >= 0) & (far_at < lax.axis_size("row"))
    strips = (
        (half, True, own, pair_rim, other_rim),
        (near_row, True, near, near_pair, near_other),
        (far_row, inside, far, far_pair, far_other),
    )
    for part in range(2):
        for row, valid, *blocks in strips:
            at = pl.ds(row, tile_r)
            mid, pair, other = (
                block[part] if valid is True else jnp.where(valid, block[part], 0.0)
                for block in blocks
            )
            ext[part, at, half : half + tile_c] = mid
            ext[part, at, pl.ds(pair_col, half)] = pair
            ext[part, at, pl.ds(other_col, half)] = other
    live_count = counts[row_place, col_place]
    probe_real, probe_imag = probe[0], probe[1]
    right_even, right_odd, left_even, left_odd = (tables.at[k] for k in range(4))
    low, high = slice(0, half), slice(half, width)
    for slot in range(slots):
        block, row_shift, lane_shift = patch_block(
            offsets, row_place, col_place, slot, half, tile_r, width
        )
        for part in range(2):
            patches[slot, part] = cut(ext[part, *block], row_shift, lane_shift)
        patch_real, patch_imag = patches[slot, 0], patches[slot, 1]
        at = slice(slot * width, (slot + 1) * width)
        for part, wave in (
            (low, probe_real * patch_real - probe_imag * patch_imag),
            (high, probe_real * patch_imag + probe_imag * patch_real),
        ):
            keep(tall_even, at, part, wave[:, low] + wave[:, high])
            keep(tall_odd, at, part, wave[:, low] - wave[:, high])
    inner = (product_of(tall_even, right_even), product_of(tall_odd, right_odd))
    for slot in range(slots):
        top = slice(slot * width, slot * width + half)
        bottom = slice(slot * width + half, (slot + 1) * width)
        for odd in range(2):
            at = slice(slot * width + odd * half, slot * width + (odd + 1) * half)
            for part in (low, high):
                upper, lower = inner[odd][top, part], inner[odd][bottom, part]
                keep(wide_even, part, at, upper + lower)
                keep(wide_odd, part, at, upper - lower)
    outer = (product_of(left_even, wide_even), product_of(left_odd, wide_odd))
    for slot in range(slots):
        lanes = slice(slot * width, (slot + 1) * width)
        for odd in range(2):
            far_real, far_imag = outer[odd][low, lanes], outer[odd][high, lanes]
            inverse = jnp.minimum(
                lax.rsqrt(far_real * far_real + far_imag * far_imag), 1.0 / modulus_floor
            )
            factor = magnitudes[slot, odd * half : (odd + 1) * half] * inverse - 1.0
            at = slice(slot * width + odd * half, slot * width + (odd + 1) * half)
            for part, back in ((low, far_real * factor), (high, far_imag * factor)):
                keep(tall_even, at, part, back[:, low])
                keep(tall_odd, at, part, back[:, high])
    inner = (product_of(tall_even, left_even), product_of(tall_odd, left_odd))
    for slot in range(slots):
        for odd, ref in enumerate((wide_even, wide_odd)):
            at = slice(slot * width + odd * half, slot * width + (odd + 1) * half)
            for part in (low, high):
                one, other = inner[0][at, part], inner[1][at, part]
                keep(ref, part, slice(slot * width, slot * width + half), one + other)
                keep(ref, part, slice(slot * width + half, (slot + 1) * width), one - other)
    outer = (product_of(right_even, wide_even), product_of(right_odd, wide_odd))
    sums = [jnp.zeros((width, width), jnp.float32)] * 3
    for slot in range(slots):
        live = jnp.where(slot < live_count, 1.0, 0.0)
        lanes = slice(slot * width, (slot + 1) * width)
        for part, rows in enumerate((low, high)):
            one, other = outer[0][rows, lanes], outer[1][rows, lanes]
            delta[slot, part, low] = (one + other) * live
            delta[slot, part, high] = (one - other) * live
        delta_real, delta_imag = delta[slot, 0], delta[slot, 1]
        patch_real, patch_imag = patches[slot, 0], patches[slot, 1]
        sums = [
            sums[0] + (patch_real * delta_real + patch_imag * delta_imag),
            sums[1] + (patch_real * delta_imag - patch_imag * delta_real),
            sums[2] + live * (patch_real * patch_real + patch_imag * patch_imag),
        ]
    even = row_odd == 0
    for layer in range(3):
        one, other = lane_groups(sums[layer])
        kept[layer * width : (layer + 1) * width] = jnp.where(even, one, other)
        given[layer * width : (layer + 1) * width] = jnp.where(even, other, one)
    total = jnp.full((SUBLANES, LANES), jnp.sum(sums[2]))
    kept[3 * width :] = total
    given[3 * width :] = total
    size = own_probe.shape[1]
    row = pl.multiple_of(lax.rem(row_place // 2, 2) * (2 * size) + col_odd * size, size)
    for part in range(2):
        one, other = lane_groups(probe[part, pl.ds(row, size), :])
        own_probe[part] = jnp.where(even, one, other)


def place_kernel(
    offsets, probe, delta, *blocks_and_ext
):
    center_mid, center_rim, packet, ext = blocks_and_ext
    slots, width = delta.shape[0], delta.shape[2]
    half = width // 2
    tile_r = center_mid.shape[1]
    tile_c = ext.shape[2] - 2 * half
    row_place = lax.axis_index("row")
    col_place = lax.axis_index("col")
    row_odd = lax.rem(row_place, 2)
    col_odd = lax.rem(col_place, 2)
    ext[...] = jnp.zeros_like(ext)
    probe_real, probe_imag = probe[0], probe[1]
    for slot in range(slots):
        real, imag = delta[slot, 0], delta[slot, 1]
        block, row_shift, lane_shift = patch_block(
            offsets, row_place, col_place, slot, half, tile_r, width
        )
        for part, grad in enumerate(
            (probe_real * real + probe_imag * imag, probe_real * imag - probe_imag * real)
        ):
            ext[part, *block] += spread(grad, row_shift, lane_shift)
    near_row = pl.multiple_of((1 - row_odd) * (tile_r + half), half)
    far_row = pl.multiple_of(row_odd * (tile_r + half), half)
    pair_col = pl.multiple_of((1 - col_odd) * (tile_c + half), half)
    other_col = pl.multiple_of(col_odd * (tile_c + half), half)
    middle = tile_c // 2
    for row, rim, mid in (
        (half, center_rim, center_mid),
        (far_row, packet.at[0:4], packet.at[4:8]),
        (near_row, packet.at[8:12], packet.at[12:16]),
    ):
        at = pl.ds(row, tile_r)
        mid[0:2] = ext[:, at, half : half + middle]
        mid[2:4] = ext[:, at, half + middle : half + tile_c]
        rim[0:2] = ext[:, at, pl.ds(pair_col, half)]
        rim[2:4] = ext[:, at, pl.ds(other_col, half)]


def stage_kernel(magnitudes, tables, ordered, held, measured, arrived):
    slots, width = magnitudes.shape[:2]
    copies = [
        pltpu.make_async_copy(tables, held, arrived.at[0]),
        pltpu.make_async_copy(magnitudes, measured, arrived.at[1]),
    ]
    for copy in copies:
        copy.start()
    line = lax.broadcasted_iota(jnp.int32, (width, width), 0)
    place = lax.broadcasted_iota(jnp.int32, (width, width), 1)

    def chosen(here, there):
        source = jnp.where(here < width // 2, 2 * here, 2 * here - (width - 1))
        return jnp.where(source == there, 1.0, 0.0).astype(jnp.bfloat16)

    by_row, by_lane = chosen(line, place), chosen(place, line)
    copies[1].wait()
    for slot in range(slots):
        rest = measured[slot]
        total = jnp.zeros((width, width), jnp.float32)
        for _ in range(3):
            piece = rest.astype(jnp.bfloat16)
            rest = rest - piece.astype(jnp.float32)
            piece = jnp.dot(by_row, piece, preferred_element_type=jnp.float32)
            total += jnp.dot(
                piece.astype(jnp.bfloat16), by_lane, preferred_element_type=jnp.float32
            )
        ordered[slot] = total
    copies[0].wait()


def stage(magnitudes):
    width = magnitudes.shape[-1]
    hbm = pl.BlockSpec(memory_space=pltpu.HBM)
    vmem = pl.BlockSpec(memory_space=pltpu.VMEM)
    return pl.pallas_call(
        stage_kernel,
        out_shape=[
            jax.ShapeDtypeStruct(magnitudes.shape, jnp.float32),
            jax.ShapeDtypeStruct((4, 2, width, width), jnp.bfloat16),
        ],
        in_specs=[hbm] * 2,
        out_specs=[vmem] * 2,
        scratch_shapes=[
            pltpu.VMEM(magnitudes.shape, jnp.float32),
            pltpu.SemaphoreType.DMA((2,)),
        ],
        compiler_params=pltpu.CompilerParams(vmem_limit_bytes=VMEM_LIMIT),
        cost_estimate=pl.CostEstimate(flops=400000000, bytes_accessed=3000000, transcendentals=0),
    )(in_hbm(magnitudes), in_hbm(jnp.asarray(dft_tables(width))))


def exit_update(offsets, counts, probe, staged, blocks):
    slots, width = staged[0].shape[:2]
    own = blocks[0]
    half = width // 2
    tile_r, tile_c = own.shape[1:]
    smem = pl.BlockSpec(memory_space=pltpu.SMEM)
    vmem = pl.BlockSpec(memory_space=pltpu.VMEM)
    return pl.pallas_call(
        delta_kernel,
        out_shape=[
            jax.ShapeDtypeStruct((3 * width + SUBLANES, LANES), jnp.float32),
            jax.ShapeDtypeStruct((3 * width + SUBLANES, LANES), jnp.float32),
            jax.ShapeDtypeStruct((2, width // 4, LANES), jnp.float32),
            jax.ShapeDtypeStruct((slots, 2, width, width), jnp.float32),
        ],
        in_specs=[smem, smem] + [vmem] * 12,
        out_specs=[vmem] * 4,
        scratch_shapes=[
            pltpu.VMEM((2, tile_r + 2 * half + SUBLANES, tile_c + 2 * half), jnp.float32),
            pltpu.VMEM((slots, 2, width, width), jnp.float32),
            pltpu.VMEM((2, slots * width, width), jnp.bfloat16),
            pltpu.VMEM((2, slots * width, width), jnp.bfloat16),
            pltpu.VMEM((2, width, slots * width), jnp.bfloat16),
            pltpu.VMEM((2, width, slots * width), jnp.bfloat16),
        ],
        compiler_params=pltpu.CompilerParams(vmem_limit_bytes=VMEM_LIMIT),
        cost_estimate=pl.CostEstimate(
            flops=3200000000, bytes_accessed=8000000, transcendentals=131072
        ),
    )(offsets, counts, probe, *map(in_vmem, staged), *map(in_vmem, blocks))


def finish_kernel(
    specimen, light, center, close, far, both, other, fresh, got, specimen_next, probe_next
):
    half = other.shape[2]
    row_place = lax.axis_index("row")
    col_place = lax.axis_index("col")
    row_odd = lax.rem(row_place, 2)
    col_odd = lax.rem(col_place, 2)
    far_at = row_place + 2 * row_odd - 1
    inside = (far_at >= 0) & (far_at < lax.axis_size("row"))
    other_at = col_place + 2 * col_odd - 1
    beside = (other_at >= 0) & (other_at < lax.axis_size("col"))
    for part in range(2):
        pair, apart = both[part], jnp.where(beside, other[part], 0.0)
        rims = (
            jnp.where(col_odd == 0, apart, pair),
            jnp.where(col_odd == 0, pair, apart),
        )
        for side, rim in enumerate(rims):
            at = slice(side * half, (side + 1) * half)
            k = 2 * side + part
            total = center[k] + close[k] + jnp.where(inside, far[k], 0.0) + rim
            specimen_next[part, :, at] = specimen[part, :, at] + total / light[:, at]
        mine, theirs = fresh[part], got[part]
        probe_next[part, :, :LANES] = jnp.where(row_odd == 0, mine, theirs)
        probe_next[part, :, LANES:] = jnp.where(row_odd == 0, theirs, mine)


def finish(specimen, probe, *values):
    vmem = pl.BlockSpec(memory_space=pltpu.VMEM)
    return pl.pallas_call(
        finish_kernel,
        out_shape=[
            jax.ShapeDtypeStruct(specimen.shape, jnp.float32),
            jax.ShapeDtypeStruct(probe.shape, jnp.float32),
        ],
        in_specs=[vmem] * (1 + len(values)),
        out_specs=[vmem] * 2,
        compiler_params=pltpu.CompilerParams(vmem_limit_bytes=VMEM_LIMIT),
        cost_estimate=pl.CostEstimate(flops=1000000, bytes_accessed=3000000, transcendentals=0),
    )(*map(in_vmem, (specimen, *values)))


def in_hbm(value):
    return pltpu.with_memory_space_constraint(value, pltpu.HBM)


def in_vmem(value):
    return pltpu.with_memory_space_constraint(value, pltpu.VMEM)


def fold_kernel(kept, got, own, across, beside, diagonal):
    layers = 3
    size = (own.shape[0] - SUBLANES) // layers
    here = 2 * lax.rem(lax.axis_index("row") // 2, 2) + lax.rem(lax.axis_index("col"), 2)
    total = kept[4 * layers * size :] + got[4 * layers * size :]
    for flip, out in enumerate((own, beside, across, diagonal)):
        row = 2 * (here // 2) + lax.rem(here, 2)
        row = (row // 2 + flip // 2) % 2 * 2 + (row % 2 + flip % 2) % 2
        for layer in range(layers):
            first = pl.multiple_of((4 * layer + row) * size, SUBLANES)
            at = pl.ds(first, size)
            out[layer * size : (layer + 1) * size] = kept[at] + got[at]
        out[layers * size :] = total


def fold(kept, got):
    vmem = pl.BlockSpec(memory_space=pltpu.VMEM)
    rows = (kept.shape[0] - SUBLANES) // 4 + SUBLANES
    return pl.pallas_call(
        fold_kernel,
        out_shape=[jax.ShapeDtypeStruct((rows, LANES), jnp.float32)] * 4,
        in_specs=[vmem] * 2,
        out_specs=[vmem] * 4,
        compiler_params=pltpu.CompilerParams(vmem_limit_bytes=VMEM_LIMIT),
        cost_estimate=pl.CostEstimate(flops=100000, bytes_accessed=400000, transcendentals=0),
    )(in_vmem(kept), in_vmem(got))


def place(offsets, probe, delta, tile_r, tile_c):
    width = probe.shape[1]
    half = width // 2
    smem = pl.BlockSpec(memory_space=pltpu.SMEM)
    vmem = pl.BlockSpec(memory_space=pltpu.VMEM)
    block = jax.ShapeDtypeStruct((4, tile_r, half), jnp.float32)
    return pl.pallas_call(
        place_kernel,
        out_shape=[block, block, jax.ShapeDtypeStruct((16, tile_r, half), jnp.float32)],
        in_specs=[smem, vmem, vmem],
        out_specs=[vmem] * 3,
        scratch_shapes=[
            pltpu.VMEM((2, tile_r + 2 * half + SUBLANES, tile_c + 2 * half), jnp.float32),
        ],
        compiler_params=pltpu.CompilerParams(vmem_limit_bytes=VMEM_LIMIT),
        cost_estimate=pl.CostEstimate(flops=4000000, bytes_accessed=4000000, transcendentals=0),
    )(offsets, probe, delta)


def exchange(value, axis, count, bit):
    return lax.ppermute(value, axis, [(i, i ^ bit) for i in range(count)])


def shards(specimen, probe_field, scan_offsets, live_counts, magnitudes):
    rows, cols = lax.axis_size("row"), lax.axis_size("col")
    width = probe_field.shape[1]
    half = width // 2
    tile_r, tile_c = specimen.shape[1:]
    row_place = lax.axis_index("row")
    col_place = lax.axis_index("col")
    row_odd = row_place % 2
    col_odd = col_place % 2
    pairs = [(i, i ^ 1) for i in range(cols)]
    others = [(i, i + 1) for i in range(1, cols - 1, 2)] + [(i + 1, i) for i in range(1, cols - 1, 2)]
    toward = [(i, i + 2) for i in range(1, rows - 2, 2)] + [(i, i - 2) for i in range(2, rows, 2)]
    toward += [(rows - 1, rows - 2), (0, 1)]
    onward_pairs = [(target, source) for source, target in toward]

    tie = lax.optimization_barrier

    def core(values):
        return [exchange(value, "row", rows, 1) for value in values]

    low, high = specimen[:, :, :half], specimen[:, :, tile_c - half :]
    pair_rim = lax.ppermute(jnp.where(col_odd == 0, high, low), "col", pairs)
    other_rim = lax.ppermute(jnp.where(col_odd == 0, low, high), "col", others)
    late, pair_rim = tie((magnitudes[0, 0], pair_rim))
    staged = stage(late)
    beyond = [lax.ppermute(block, "row", toward) for block in (specimen, pair_rim)]
    other_rim, staged, beyond = tie((other_rim, staged, beyond))
    own = [specimen, pair_rim, other_rim]
    beyond += [lax.ppermute(other_rim, "row", toward)]
    probe_late, other_rim = tie((probe_field, other_rim))
    light = lighting(scan_offsets, live_counts, probe_late, tile_r, tile_c)
    beyond[2], light = tie((beyond[2], light))
    far_rims = core([jnp.concatenate(beyond[1:])])[0]
    far = [*core(beyond[:1]), far_rims[:2], far_rims[2:]]
    kept, given, own_probe, delta = exit_update(
        scan_offsets, live_counts, probe_field, staged, own + core(own) + far
    )

    def pick(condition, first, second):
        return jnp.where(condition, first, second)

    square = [
        (r * cols + c, (r ^ 2) * cols + (c ^ 1)) for r in range(rows) for c in range(cols)
    ]

    def all_three(across, beside, diagonal):
        diagonal = lax.ppermute(diagonal, ("row", "col"), square)
        return exchange(across, "row", rows, 2), exchange(beside, "col", cols, 1), diagonal

    got = exchange(given, "row", rows, 1)
    center_mid, center_rim, packet = place(scan_offsets, probe_field, delta, tile_r, tile_c)
    got, packet = tie((got, packet))
    packet = exchange(packet, "row", rows, 1)
    value, across, beside, diagonal = fold(kept, got)
    beyond_rim = lax.ppermute(packet[:4], "row", onward_pairs)
    beyond_mid = lax.ppermute(packet[4:8], "row", onward_pairs)
    across, beside, diagonal = all_three(across, beside, diagonal)
    value = (value + across) + (beside + diagonal)
    value, beyond_rim = tie((value, beyond_rim))
    inside = (row_place + 2 * row_odd - 1 >= 0) & (row_place + 2 * row_odd - 1 < rows)
    rim = center_rim + packet[8:12] + pick(inside, beyond_rim, 0.0)
    pair_part = rim[:2]
    other_part = lax.ppermute(rim[2:], "col", others + [(0, cols - 1), (cols - 1, 0)])
    value = value + exchange(value, "col", cols, 2)
    for bit in (1 << k for k in range(2, cols.bit_length() - 1)):
        value = value + exchange(value, "col", cols, 2 * bit - 2)
    for bit in (1 << k for k in range(2, rows.bit_length() - 1)):
        value = value + exchange(value, "row", rows, bit)
    value, other_part, pair_part, beyond_mid = tie(
        (value, other_part, pair_part, beyond_mid)
    )
    size = own_probe.shape[1]
    real, imag, weight, total = (value[k * size : (k + 1) * size] for k in range(4))
    update = jnp.stack([real, imag]) / (weight + probe_damping * (total[:1] / (width * width)))
    fresh = own_probe + update
    size = fresh.size // LANES
    both = jnp.concatenate([fresh.reshape(size, LANES), pair_part.reshape(-1, LANES)])
    across, both, diagonal = all_three(fresh, both, fresh)
    beside = both[:size].reshape(fresh.shape)
    pair_part = both[size:].reshape(pair_part.shape)

    def ordered(place_here, one, other):
        return pick(
            place_here == 0,
            jnp.concatenate([one, other], 1),
            jnp.concatenate([other, one], 1),
        )

    fresh = ordered(
        (row_place // 2) % 2, ordered(col_odd, fresh, beside), ordered(col_odd, across, diagonal)
    )
    got = exchange(fresh, "row", rows, 1)
    return finish(
        specimen, probe_field, light, center_mid, packet[12:], beyond_mid,
        pair_part, other_part, fresh, got,
    )


def solution(mesh):
    return jax.shard_map(
        shards,
        mesh=mesh,
        in_specs=(P(None, "row", "col"), P(), P(), P(), P("row", "col", None, None, None)),
        out_specs=(P(None, "row", "col"), P()),
        check_vma=False,
    )
```
